256 devices in a mesh: tm: 16 (over z, core), vocab: 16 (over y, x).
Axes of the slice: x: 4, y: 4, z: 8, core: 2. Of those that a mesh axis runs over, the one named last changes fastest.
Arguments:
- counts: int32 [64, 2048, 2048], P('tm', 'vocab'), may hold values from 0 to 5
- word_vecs: bfloat16 [64, 2048, 200], P('tm', 'vocab'), may hold values from -1.796875 to 1.796875
- ctx_vecs: bfloat16 [64, 2048, 200], P('tm', 'vocab'), may hold values from -1.796875 to 1.796875
- gaps: int32 [64], replicated, may hold values from 1 to 4
Outputs:
- new_words: bfloat16 [64, 2048, 200], P('tm', 'vocab')
- new_contexts: bfloat16 [64, 2048, 200], P('tm', 'vocab')
- drift: float32 [64, 2048], P('tm', 'vocab')
The draws below stay inside these ranges and needn't reach their ends.
All inputs are finite; a program needn't handle non-finite values.
Results may differ from the reference program's by a relative error of at most 0.02.
Values may be sent and summed in bfloat16 or wider, within the bound.
No kernel may reach another device: no remote copies, remote signals or barrier semaphores. Data moves between devices by JAX's collectives and lax.ppermute only.
A program may use at most 64 MiB of HBM per device.

```python
import jax
import jax.numpy as jnp
from jax import lax

E = 200
SWEEPS = 2
VOCAB = 2048
YEARS = 64


def with_ends(values, rng, smallest, top_value):
    longest = values.shape.index(max(values.shape))
    spots = []
    for shift in (0, 1):
        where = [jax.random.randint(jax.random.fold_in(rng, axis), (), 0, length) for axis, length in enumerate(values.shape)]
        where[longest] = (where[longest] + shift) % values.shape[longest]
        spots.append(tuple(where))
    return values.at[spots[0]].set(smallest).at[spots[1]].set(top_value)


def levels(rng, shape, cuts, low, top_value):
    def one(dim, shards_of):
        heights = jax.random.uniform(jax.random.fold_in(jax.random.fold_in(rng, 6), dim), (shards_of,), jnp.float32, low / len(cuts), top_value / len(cuts))
        return jnp.repeat(jnp.exp(heights), shape[dim] // shards_of).reshape((-1,) + (1,) * (len(shape) - dim - 1))

    level = one(*cuts[0])
    for cut in cuts[1:]:
        level = level * one(*cut)
    return level


def noise(rng, dims, width, limit, split=(), held_as=jnp.bfloat16):
    result = jax.random.normal(rng, dims, jnp.float32) * width
    if len(split) > 0:
        result = levels(rng, dims, split, -0.22, 0.18) * result
    return jnp.clip(result, min=-limit, max=limit).astype(held_as)


def setup_inputs(seed: int = 0) -> dict:
    key_list = jax.random.split(jax.random.key(seed), 5)
    counts = with_ends(jax.random.randint(key_list[0], (YEARS, VOCAB, VOCAB), 0, 6), jax.random.fold_in(key_list[0], 1), 0, 5).astype(jnp.int32)
    word_vecs = noise(key_list[1], (YEARS, VOCAB, E), 0.3, 1.796875, ((0, 16), (1, 16)))
    ctx_vecs = noise(key_list[2], (YEARS, VOCAB, E), 0.3, 1.796875, ((0, 16), (1, 16)))
    gaps = with_ends(jax.random.randint(key_list[3], (YEARS,), 1, 5), jax.random.fold_in(key_list[3], 1), 1, 4).astype(jnp.int32)
    return dict(counts=counts, word_vecs=word_vecs, ctx_vecs=ctx_vecs, gaps=gaps)


PRIOR = 0.05
DIFF = 0.5
RATE = 0.2

def jensen(first, second):
    lp = jax.nn.log_sigmoid(first)
    lq = jax.nn.log_sigmoid(second)
    lnp = jax.nn.log_sigmoid(-first)
    lnq = jax.nn.log_sigmoid(-second)
    half = jnp.log(2.0)
    mean_one = jnp.logaddexp(lp, lq) - half
    mean_zero = jnp.logaddexp(lnp, lnq) - half
    return 0.5 * (jnp.exp(lp) * (lp - mean_one) + jnp.exp(lnp) * (lnp - mean_zero) + jnp.exp(lq) * (lq - mean_one) + jnp.exp(lnq) * (lnq - mean_zero))

def reference(counts, word_vecs, ctx_vecs, gaps):
    rates = 1.0 / (DIFF * gaps.astype(jnp.float32))
    link = rates[:-1]
    zero = jnp.zeros((1,), jnp.float32)
    diagonal = PRIOR + jnp.concatenate([zero, link]) + jnp.concatenate([link, zero])
    precision = jnp.diag(diagonal) - jnp.diag(link, 1) - jnp.diag(link, -1)
    scale = RATE / jnp.sqrt(jnp.float32(VOCAB))
    words, contexts = (word_vecs, ctx_vecs)

    def gradients(item):
        count_t, word_t, ctx_t = item
        weights = count_t.astype(jnp.float32)
        negative = lax.optimization_barrier(jnp.sum(weights, axis=1, keepdims=True)) / VOCAB
        scores = jnp.dot(word_t.astype(jnp.float32), ctx_t.T.astype(jnp.float32), preferred_element_type=jnp.float32)
        sig = jax.nn.sigmoid(scores)
        coeff = (weights * (1.0 - sig) - negative * sig).astype(jnp.bfloat16)
        return (jnp.dot(coeff.astype(jnp.float32), ctx_t.astype(jnp.float32), preferred_element_type=jnp.float32), jnp.dot(coeff.T.astype(jnp.float32), word_t.astype(jnp.float32), preferred_element_type=jnp.float32))

    def divergence(item):
        word_t, ctx_t, word_n, ctx_n = item
        scores = jnp.dot(word_t.astype(jnp.float32), ctx_t.T.astype(jnp.float32), preferred_element_type=jnp.float32)
        following = jnp.dot(word_n.astype(jnp.float32), ctx_n.T.astype(jnp.float32), preferred_element_type=jnp.float32)
        return lax.optimization_barrier(jnp.sum(jensen(scores, following), axis=1)) / jnp.sqrt(jnp.float32(VOCAB))
    drift = None
    for sweep in range(SWEEPS):
        if sweep == 0:
            raw = lax.map(divergence, (words, contexts, jnp.roll(words, -1, 0), jnp.roll(contexts, -1, 0)))
            years = jnp.arange(YEARS)
            drift = jnp.where((years == YEARS - 1)[:, None], jnp.zeros_like(raw), raw)
        word_grad, ctx_grad = lax.map(gradients, (counts, words, contexts))
        stacked = jnp.stack([word_grad, ctx_grad], 1).reshape(YEARS, -1)
        solved = jnp.linalg.solve(precision, stacked).reshape(YEARS, 2, VOCAB, E)
        words = (words.astype(jnp.float32) + scale * solved[:, 0]).astype(jnp.bfloat16)
        contexts = (contexts.astype(jnp.float32) + scale * solved[:, 1]).astype(jnp.bfloat16)
    return (words, contexts, drift)
```

```python
import functools

import jax
import jax.numpy as jnp
from jax import lax
from jax.experimental import pallas as pl
from jax.experimental.pallas import tpu as pltpu
from jax.sharding import PartitionSpec as P

PRIOR = 0.05
DIFF = 0.5
RATE = 0.2
SWEEPS = 2


E = 200
EP = 208
B = 128
T = 4
Q = 4
F32 = jnp.float32
BF16 = jnp.bfloat16

PARAMS = functools.partial(pltpu.CompilerParams, vmem_limit_bytes=24 * 1024 * 1024)


def sds(shape, dtype):
    return jax.ShapeDtypeStruct(shape, dtype)


def vmem():
    return pl.BlockSpec(memory_space=pltpu.VMEM)


def year_block(*dims):
    return pl.BlockSpec((1, *dims), lambda t: (t,) + (0,) * len(dims))


def cost(flops, moved, special=0):
    return pl.CostEstimate(flops=int(flops), bytes_accessed=int(moved), transcendentals=int(special))


def stage_kernel(counts_ref, words_ref, ctx_ref, *outs):
    tiles, (wt_ref, ct_ref) = outs[:Q], outs[Q:]
    place = lax.axis_index("vocab")
    y, x = place // Q, place % Q
    counts = counts_ref[0].astype(F32).astype(BF16)
    ones = jnp.ones((8, counts.shape[1]), BF16)
    total = lax.dot_general(ones, counts, (((1,), (1,)), ((), ())), preferred_element_type=F32)
    high = total.astype(BF16).astype(F32)
    rest = total - high
    row = lax.broadcasted_iota(jnp.int32, (8, B), 0)
    spare = jnp.where(row == 0, high, jnp.where(row == 1, rest, 0.0))
    wt_ref[0] = jnp.concatenate([words_ref[0].astype(F32).T, spare], 0).astype(BF16)
    ct_ref[0] = jnp.concatenate([ctx_ref[0].astype(F32).T, jnp.zeros((8, B), F32)], 0).astype(BF16)
    for s in range(Q):
        for j in range(Q):
            block = ((y + Q - j) % Q) * Q + (x + s) % Q
            at = pl.multiple_of(block * B, B)
            tiles[s][0, :, j * B : (j + 1) * B] = (
                counts_ref[0, :, pl.ds(at, B)].astype(F32).astype(BF16)
            )


def stage(counts, words, contexts):
    vocab = counts.shape[2]
    return pl.pallas_call(
        stage_kernel,
        grid=(T,),
        in_specs=[year_block(B, vocab), year_block(B, E), year_block(B, E)],
        out_specs=[year_block(B, Q * B)] * Q + [year_block(EP, B)] * 2,
        out_shape=[sds((T, B, Q * B), BF16)] * Q + [sds((T, EP, B), BF16)] * 2,
        compiler_params=PARAMS(),
        cost_estimate=cost(T * B * vocab * 16, T * B * vocab * 6),
        name="stage",
    )(counts, words, contexts)


def coefficient_kernel(gaps_ref, out_ref, link_ref, f_ref, g_ref, d_ref, e_ref, a_ref, c_ref):
    years = gaps_ref.shape[0]
    chips = years // (2 * T)
    one = jnp.ones((1, B), F32)
    zero = jnp.zeros((1, B), F32)
    for t in range(years - 1):
        link_ref[t : t + 1] = one / (DIFF * (one * gaps_ref[t].astype(F32)))

    def link(t):
        return link_ref[t : t + 1] if 0 <= t < years - 1 else zero

    def diagonal(t):
        return PRIOR + link(t - 1) + link(t)

    delta, eps = diagonal(0), diagonal(years - 1)
    f_ref[0:1] = zero
    g_ref[years - 1 : years] = zero
    d_ref[0:1] = delta
    e_ref[years - 1 : years] = eps
    for t in range(1, years):
        f = link(t - 1) / delta
        delta = diagonal(t) - link(t - 1) * f
        f_ref[t : t + 1] = f
        d_ref[t : t + 1] = delta
        u = years - 1 - t
        g = link(u) / eps
        eps = diagonal(u) - link(u) * g
        g_ref[u : u + 1] = g
        e_ref[u : u + 1] = eps
    for t in range(years):
        d_ref[t : t + 1] = one / (d_ref[t : t + 1] + e_ref[t : t + 1] - diagonal(t))
    for k in range(2 * chips):
        fs, gs = f_ref[k * T : k * T + 1], g_ref[k * T : k * T + 1]
        for j in range(1, T):
            fs = fs * f_ref[k * T + j : k * T + j + 1]
            gs = gs * g_ref[k * T + j : k * T + j + 1]
        a_ref[k : k + 1] = fs
        c_ref[k : k + 1] = gs
    k = lax.axis_index("tm")
    z = k // 2
    for j in range(T):
        out_ref[j : j + 1] = f_ref[pl.ds(k * T + j, 1)]
        out_ref[T + j : T + j + 1] = g_ref[pl.ds(k * T + j, 1)]
        out_ref[2 * T + j : 2 * T + j + 1] = d_ref[pl.ds(k * T + j, 1)]
    out_ref[12:13] = a_ref[pl.ds(2 * z, 1)]
    out_ref[13:14] = a_ref[pl.ds(2 * z + 1, 1)]
    out_ref[14:15] = c_ref[pl.ds(2 * z, 1)]
    out_ref[15:16] = c_ref[pl.ds(2 * z + 1, 1)]
    out_ref[16:17] = zero
    forward, backward = one, one
    for d in range(1, chips):
        out_ref[16 + d : 17 + d] = forward
        out_ref[24 + d : 25 + d] = backward
        earlier = jnp.maximum(z - d, 0)
        later = jnp.minimum(z + d, chips - 1)
        forward = forward * a_ref[pl.ds(2 * earlier, 1)] * a_ref[pl.ds(2 * earlier + 1, 1)]
        backward = backward * c_ref[pl.ds(2 * later, 1)] * c_ref[pl.ds(2 * later + 1, 1)]
    out_ref[24:25] = zero


def coefficients(gaps):
    years = gaps.shape[0]
    return pl.pallas_call(
        coefficient_kernel,
        in_specs=[pl.BlockSpec(memory_space=pltpu.SMEM)],
        out_specs=vmem(),
        out_shape=sds((32, B), F32),
        scratch_shapes=[pltpu.VMEM((years, B), F32)] * 5 + [pltpu.VMEM((16, B), F32)] * 2,
        compiler_params=PARAMS(),
        cost_estimate=cost(years * B * 200, years * 600),
        name="coefficients",
    )(gaps)


def gradient_kernel(with_drift, *refs):
    w, c, n = refs[0:Q], refs[Q : 2 * Q], refs[2 * Q : 3 * Q]
    refs = refs[3 * Q :]
    if with_drift:
        drift_ref, refs = refs[0], refs[1:]
    gw, gc, coeff_ref = refs[:Q], refs[Q : 2 * Q], refs[2 * Q]
    vocab = Q * Q * B
    panel = jnp.concatenate([r[0] for r in c], 1)
    for i in range(Q):
        block = w[i][0].astype(F32).T
        negative = (block[:, E : E + 1] + block[:, E + 1 : E + 2]) * (1.0 / vocab)
        scores = jnp.dot(block.astype(BF16), panel, preferred_element_type=F32)
        sig = 1.0 / (1.0 + jnp.exp(-scores))
        weights = n[i][0].astype(F32)
        coeff_ref[i * B : (i + 1) * B, :] = (weights * (1.0 - sig) - negative * sig).astype(BF16)
    coeff = coeff_ref[...]
    word_grad = lax.dot_general(panel, coeff, (((1,), (1,)), ((), ())), preferred_element_type=F32)
    words = jnp.concatenate([r[0] for r in w], 1)
    ctx_grad = jnp.dot(words, coeff, preferred_element_type=F32)
    if with_drift:
        word_grad = jnp.concatenate([word_grad[:E], drift_ref[0]], 0)
    word_grad = word_grad.astype(BF16)
    ctx_grad = ctx_grad.astype(BF16)
    for i in range(Q):
        gw[i][0] = word_grad[:, i * B : (i + 1) * B]
        gc[i][0] = ctx_grad[:, i * B : (i + 1) * B]


def gradients(w, c, n, drift=None):
    block = year_block(EP, B)
    with_drift = drift is not None
    return pl.pallas_call(
        functools.partial(gradient_kernel, with_drift),
        grid=(T,),
        in_specs=[block] * (2 * Q)
        + [year_block(B, Q * B)] * Q
        + ([year_block(8, Q * B)] if with_drift else []),
        out_specs=[block] * (2 * Q),
        out_shape=[sds((T, EP, B), BF16)] * (2 * Q),
        scratch_shapes=[pltpu.VMEM((Q * B, Q * B), BF16)],
        compiler_params=PARAMS(),
        cost_estimate=cost(6 * T * 512 * 512 * EP, 6 << 20, 2 * T * 512 * 512),
        name="gradients",
    )(*w, *c, *n, *([drift] if with_drift else []))


def entropy(scores):
    size = jnp.abs(scores)
    small = jnp.exp(-size)
    upper = 1.0 / (1.0 + small)
    lower = small * upper
    return jnp.where(scores >= 0, upper, lower), jnp.log(upper) - lower * size


def drift_kernel(*refs):
    w, c, following, out_ref = refs[0:Q], refs[Q : 2 * Q], refs[2 * Q], refs[2 * Q + 1]
    p_ref, h_ref = refs[2 * Q + 2 :]
    i = pl.program_id(0)
    tiny = jnp.finfo(F32).tiny

    def sweep(which):
        for t in range(T + 1):
            if t < T:
                panel = jnp.concatenate([r[t] for r in c], 1)
                block = w[which][t]
            else:
                panel = jnp.concatenate([following[Q + j] for j in range(Q)], 1)
                block = following[which]
            scores = jnp.dot(block.astype(F32).T.astype(BF16), panel, preferred_element_type=F32)
            p, h = entropy(scores)
            if t > 0:
                before = p_ref[...]
                m = 0.5 * (before + p)
                n = 1.0 - m
                mixed = m * jnp.log(jnp.maximum(m, tiny)) + n * jnp.log(jnp.maximum(n, tiny))
                js = 0.5 * (h_ref[...] + h) - mixed
                total = js[:, :B] + js[:, B : 2 * B] + js[:, 2 * B : 3 * B] + js[:, 3 * B :]
                total = jnp.sum(total.T, axis=0, keepdims=True)
                high = total.astype(BF16).astype(F32)
                row = lax.broadcasted_iota(jnp.int32, (8, B), 0)
                out_ref[t - 1, :, which * B : (which + 1) * B] = jnp.where(
                    row == 0, high, jnp.where(row == 1, total - high, 0.0)
                )
            if t < T:
                p_ref[...] = p
                h_ref[...] = h

    del i
    for which in range(Q):
        sweep(which)


def drift_parts(w, c, following):
    return pl.pallas_call(
        drift_kernel,
        grid=(1,),
        in_specs=[vmem()] * (2 * Q + 1),
        out_specs=vmem(),
        out_shape=sds((T, 8, Q * B), F32),
        scratch_shapes=[pltpu.VMEM((B, Q * B), F32)] * 2,
        compiler_params=PARAMS(),
        cost_estimate=cost(2 * 5 * 512 * 512 * (EP + 30), 4 << 20, 5 * 5 * 512 * 512),
        name="drift",
    )(*w, *c, following)


def summary_kernel(*refs):
    parts = (refs[0:Q], refs[Q : 2 * Q])
    co_ref = refs[2 * Q]
    b_ref, keep_ref, send_ref = refs[2 * Q + 1 :]
    odd = lax.axis_index("tm") % 2
    for q in range(2):
        for t in range(T):
            total = parts[q][0][t].astype(F32)
            for r in parts[q][1:]:
                total = total + r[t].astype(F32)
            b_ref[q, t] = total
        forward = b_ref[q, 0]
        for t in range(1, T):
            forward = b_ref[q, t] + co_ref[t : t + 1] * forward
        backward = b_ref[q, T - 1]
        for t in reversed(range(T - 1)):
            backward = b_ref[q, t] + co_ref[T + t : T + t + 1] * backward

        @pl.when(odd == q)
        def _():
            keep_ref[0] = forward
            keep_ref[1] = backward

        @pl.when(odd != q)
        def _():
            send_ref[0] = forward
            send_ref[1] = backward


def summaries(gw, gc, co):
    return pl.pallas_call(
        summary_kernel,
        in_specs=[vmem()] * (2 * Q + 1),
        out_specs=[vmem()] * 3,
        out_shape=[sds((2, T, EP, B), F32)] + [sds((2, EP, B), F32)] * 2,
        compiler_params=PARAMS(),
        cost_estimate=cost(2 * T * EP * B * 10, 3 << 20),
        name="summaries",
    )(*gw, *gc, co)


def pair(own_ref, other_ref, which, odd):
    own, other = own_ref[which], other_ref[which]
    return jnp.where(odd == 0, own, other), jnp.where(odd == 0, other, own)


def chip_kernel(own_ref, other_ref, co_ref, *outs):
    k = lax.axis_index("tm")
    odd, z = k % 2, k // 2
    chips = len(outs) + 1
    even_f, odd_f = pair(own_ref, other_ref, 0, odd)
    even_b, odd_b = pair(own_ref, other_ref, 1, odd)
    forward = (odd_f + co_ref[13:14] * even_f).astype(BF16)
    backward = (even_b + co_ref[14:15] * odd_b).astype(BF16)
    for d in range(1, chips):

        @pl.when(z + d < chips)
        def _(d=d):
            outs[d - 1][...] = forward

        @pl.when(z + d >= chips)
        def _(d=d):
            outs[d - 1][...] = backward


def chip_summaries(own, other, co, chips):
    return pl.pallas_call(
        chip_kernel,
        in_specs=[vmem()] * 3,
        out_specs=[vmem()] * (chips - 1),
        out_shape=[sds((EP, B), BF16)] * (chips - 1),
        compiler_params=PARAMS(),
        cost_estimate=cost(EP * B * 16, 1 << 20),
        name="chip_summaries",
    )(own, other, co)


def incoming_kernel(*refs):
    *got, own_ref, other_ref, co_ref, mine_ref, send_ref, y_ref, z_ref = refs
    k = lax.axis_index("tm")
    odd, z = k % 2, k // 2
    chips = len(got) + 1
    y_ref[...] = jnp.zeros_like(y_ref)
    z_ref[...] = jnp.zeros_like(z_ref)
    for d in range(1, chips):

        @pl.when(z >= d)
        def _(d=d):
            y_ref[...] += co_ref[16 + d : 17 + d] * got[d - 1][...].astype(F32)

        @pl.when(z < d)
        def _(d=d):
            z_ref[...] += co_ref[24 + chips - d : 25 + chips - d] * got[d - 1][...].astype(F32)

    even_f, _ = pair(own_ref, other_ref, 0, odd)
    _, odd_b = pair(own_ref, other_ref, 1, odd)
    y_even = y_ref[...]
    y_odd = even_f + co_ref[12:13] * y_even
    z_odd = z_ref[...]
    z_even = odd_b + co_ref[15:16] * z_odd
    mine_ref[0] = jnp.where(odd == 0, y_even, y_odd)
    mine_ref[1] = jnp.where(odd == 0, z_even, z_odd)
    send_ref[0] = jnp.where(odd == 0, y_odd, y_even)
    send_ref[1] = jnp.where(odd == 0, z_odd, z_even)


def incoming(got, own, other, co):
    return pl.pallas_call(
        incoming_kernel,
        in_specs=[vmem()] * (len(got) + 3),
        out_specs=[vmem()] * 2,
        out_shape=[sds((2, EP, B), F32)] * 2,
        scratch_shapes=[pltpu.VMEM((EP, B), F32)] * 2,
        compiler_params=PARAMS(),
        cost_estimate=cost(EP * B * 30, 1 << 20),
        name="incoming",
    )(*got, own, other, co)


def solved_years(b_ref, q, y, z, co_ref):
    ys = []
    for t in range(T):
        y = b_ref[q, t] + co_ref[t : t + 1] * y
        ys.append(y)
    out = [None] * T
    for t in reversed(range(T)):
        carried = co_ref[T + t : T + t + 1] * z
        z = b_ref[q, t] + carried
        out[t] = (ys[t] + carried) * co_ref[2 * T + t : 2 * T + t + 1]
    return out


def pick(mine_ref, other_ref, odd, q, which):
    return jnp.where(odd == q, mine_ref[which], other_ref[which])


def update_kernel(scale, b_ref, mine_ref, other_ref, co_ref, w_ref, c_ref, nw_ref, nc_ref):
    odd = lax.axis_index("tm") % 2
    live = lax.broadcasted_iota(jnp.int32, (EP, B), 0) < E
    for q, (old, new) in enumerate(((w_ref, nw_ref), (c_ref, nc_ref))):
        y = pick(mine_ref, other_ref, odd, q, 0)
        z = pick(mine_ref, other_ref, odd, q, 1)
        solved = solved_years(b_ref, q, y, z, co_ref)
        for t in range(T):
            new[t] = (old[t].astype(F32) + jnp.where(live, scale * solved[t], 0.0)).astype(BF16)


def finish_kernel(scale, vocab, b_ref, mine_ref, other_ref, co_ref, w_ref, c_ref, nw_ref, nc_ref, dr_ref):
    k = lax.axis_index("tm")
    odd, last = k % 2, k == lax.axis_size("tm") - 1
    for q, (old, new) in enumerate(((w_ref, nw_ref), (c_ref, nc_ref))):
        y = pick(mine_ref, other_ref, odd, q, 0)
        z = pick(mine_ref, other_ref, odd, q, 1)
        solved = solved_years(b_ref, q, y, z, co_ref)
        for t in range(T):
            fresh = old[t].astype(F32) + scale * solved[t]
            new[t] = fresh[:E].T.astype(BF16)
    for t in range(T):
        total = (b_ref[0, t, E : E + 1] + b_ref[0, t, E + 1 : E + 2]) * (float(vocab) ** -0.5)
        if t == T - 1:
            total = jnp.where(last, jnp.zeros_like(total), total)
        dr_ref[t : t + 1] = total


def update(scale, b, mine, other, co, words, contexts):
    return pl.pallas_call(
        functools.partial(update_kernel, scale),
        in_specs=[vmem()] * 6,
        out_specs=[vmem()] * 2,
        out_shape=[sds((T, EP, B), BF16)] * 2,
        compiler_params=PARAMS(),
        cost_estimate=cost(2 * T * EP * B * 10, 3 << 20),
        name="update",
    )(b, mine, other, co, words, contexts)


def finish(scale, vocab, b, mine, other, co, words, contexts):
    return pl.pallas_call(
        functools.partial(finish_kernel, scale, vocab),
        in_specs=[vmem()] * 6,
        out_specs=[vmem()] * 3,
        out_shape=[sds((T, B, E), BF16)] * 2 + [sds((T, B), F32)],
        compiler_params=PARAMS(),
        cost_estimate=cost(2 * T * EP * B * 10, 3 << 20),
        name="finish",
    )(b, mine, other, co, words, contexts)


def along_x(a, s):
    pairs = [(y * Q + x, y * Q + (x + s) % Q) for y in range(Q) for x in range(Q)]
    return lax.ppermute(a, "vocab", pairs)


def along_y(a, s):
    pairs = [(y * Q + x, ((y + s) % Q) * Q + x) for y in range(Q) for x in range(Q)]
    return lax.ppermute(a, "vocab", pairs)


def other_core(a):
    return lax.ppermute(a, "tm", [(k, k ^ 1) for k in range(lax.axis_size("tm"))])


def along_z(a, d):
    chips = lax.axis_size("tm") // 2
    pairs = [(2 * z + core, 2 * ((z + d) % chips) + core) for z in range(chips) for core in range(2)]
    return lax.ppermute(a, "tm", pairs)


def from_next(a):
    return lax.ppermute(a, "tm", [(k, k - 1) for k in range(1, lax.axis_size("tm"))])


def gathered(words, contexts):
    w = [words] + [along_x(words, s) for s in range(1, Q)]
    c = [contexts] + [along_y(contexts, s) for s in range(1, Q)]
    return w, c


def on_device(counts, word_vecs, ctx_vecs, gaps):
    vocab = counts.shape[2]
    chips = lax.axis_size("tm") // 2
    scale = RATE / float(vocab) ** 0.5
    *tiles, words, contexts = stage(counts, word_vecs, ctx_vecs)
    co = coefficients(gaps)
    w, c = gathered(words, contexts)
    n = [tiles[0]] + [along_x(tiles[s], s) for s in range(1, Q)]
    following = from_next(jnp.stack([a[0] for a in w + c], 0))
    parts = drift_parts(w, c, following)
    for sweep in range(SWEEPS):
        last = sweep == SWEEPS - 1
        if sweep:
            w, c = gathered(words, contexts)
        grads = gradients(w, c, n, parts if last else None)
        gw = [grads[0]] + [along_x(grads[s], -s) for s in range(1, Q)]
        gc = [grads[Q]] + [along_y(grads[Q + s], -s) for s in range(1, Q)]
        b, own, send = summaries(gw, gc, co)
        other = other_core(send)
        outs = chip_summaries(own, other, co, chips)
        got = [along_z(outs[d - 1], d) for d in range(1, chips)]
        mine, send = incoming(got, own, other, co)
        other = other_core(send)
        if last:
            return tuple(finish(scale, vocab, b, mine, other, co, words, contexts))
        words, contexts = update(scale, b, mine, other, co, words, contexts)


def solution(mesh):
    return jax.shard_map(
        on_device,
        mesh=mesh,
        in_specs=(P("tm", "vocab", None), P("tm", "vocab", None), P("tm", "vocab", None), P()),
        out_specs=(P("tm", "vocab", None), P("tm", "vocab", None), P("tm", "vocab")),
        check_vma=False,
    )
```

```python
import functools

import jax
import jax.numpy as jnp
from jax import lax
from jax.experimental import pallas as pl
from jax.experimental.pallas import tpu as pltpu
from jax.sharding import PartitionSpec as P

PRIOR = 0.05
DIFF = 0.5
RATE = 0.2
SWEEPS = 2


E = 200
EP = 208
B = 128
T = 4
Q = 4
HALF = 4
F32 = jnp.float32
BF16 = jnp.bfloat16

PARAMS = functools.partial(pltpu.CompilerParams, vmem_limit_bytes=24 * 1024 * 1024)


def sds(shape, dtype):
    return jax.ShapeDtypeStruct(shape, dtype)


def vmem():
    return pl.BlockSpec(memory_space=pltpu.VMEM)


def cost(flops, moved, special=0):
    return pl.CostEstimate(flops=int(flops), bytes_accessed=int(moved), transcendentals=int(special))


COUNT_ROWS = T * Q * B
ROWS = COUNT_ROWS + T * EP


def count_block(ref, t, j):
    at = (t * Q + j) * B
    return ref[at : at + B]


def word_block(ref, t):
    at = COUNT_ROWS + t * EP
    return ref[at : at + EP]


def stage_kernel(counts_hbm, w_ref, c_ref, *refs):
    loads, (ctx_ref, first_ref, held_ref, sems) = refs[:Q], refs[Q:]
    along_rows = lax.axis_index("tm") % 2 == 0
    place = lax.axis_index("vocab")
    y, x = place // Q, place % Q
    copies = [pltpu.make_async_copy(counts_hbm.at[t], held_ref.at[t], sems.at[t]) for t in range(T)]
    for copy in copies:
        copy.start()
    row = lax.broadcasted_iota(jnp.int32, (8, B), 0)
    zero = jnp.zeros((8, B), F32)
    ones = jnp.ones((8, counts_hbm.shape[2]), BF16)
    for t in range(T):
        context = jnp.concatenate([c_ref[t].astype(F32), zero], 0).astype(BF16)
        ctx_ref[t] = context
        copies[t].wait()
        counts = held_ref[t].astype(F32).astype(BF16)
        total = lax.dot_general(ones, counts, (((1,), (1,)), ((), ())), preferred_element_type=F32)
        high = total.astype(BF16).astype(F32)
        spare = jnp.where(row == 0, high, jnp.where(row == 1, total - high, 0.0))
        word = jnp.concatenate([w_ref[t].astype(F32), spare], 0).astype(BF16)
        if t == 0:
            first_ref[0] = word
            first_ref[1] = context
        for s in range(Q):
            loads[s][COUNT_ROWS + t * EP : COUNT_ROWS + (t + 1) * EP] = word
            for j in range(Q):
                block = jnp.where(
                    along_rows,
                    ((y + Q - j) % Q) * Q + (x + s) % Q,
                    ((y + s) % Q) * Q + (x + Q - j) % Q,
                )
                at = pl.multiple_of(block * B, B)
                to = (t * Q + j) * B
                loads[s][to : to + B] = held_ref[t, :, pl.ds(at, B)].astype(F32).astype(BF16)


def stage(counts, words, contexts):
    vocab = counts.shape[2]
    return pl.pallas_call(
        stage_kernel,
        in_specs=[pl.BlockSpec(memory_space=pltpu.HBM), vmem(), vmem()],
        out_specs=[vmem()] * (Q + 2),
        out_shape=[sds((ROWS, B), BF16)] * Q + [sds((T, EP, B), BF16), sds((2, EP, B), BF16)],
        scratch_shapes=[pltpu.VMEM((T, B, vocab), jnp.int32), pltpu.SemaphoreType.DMA((T,))],
        compiler_params=PARAMS(),
        cost_estimate=cost(T * B * vocab * 16, T * B * vocab * 6),
        name="stage",
    )(counts, words, contexts)


def coefficient_kernel(gaps_ref, out_ref, link_ref, f_ref, g_ref, d_ref, e_ref, a_ref, c_ref):
    years = gaps_ref.shape[0]
    chips = years // (2 * T)
    one = jnp.ones((1, B), F32)
    zero = jnp.zeros((1, B), F32)
    for t in range(years - 1):
        link_ref[t : t + 1] = one / (DIFF * (one * gaps_ref[t].astype(F32)))

    def link(t):
        return link_ref[t : t + 1] if 0 <= t < years - 1 else zero

    def diagonal(t):
        return PRIOR + link(t - 1) + link(t)

    delta, eps = diagonal(0), diagonal(years - 1)
    f_ref[0:1] = zero
    g_ref[years - 1 : years] = zero
    d_ref[0:1] = delta
    e_ref[years - 1 : years] = eps
    for t in range(1, years):
        f = link(t - 1) / delta
        delta = diagonal(t) - link(t - 1) * f
        f_ref[t : t + 1] = f
        d_ref[t : t + 1] = delta
        u = years - 1 - t
        g = link(u) / eps
        eps = diagonal(u) - link(u) * g
        g_ref[u : u + 1] = g
        e_ref[u : u + 1] = eps
    for t in range(years):
        d_ref[t : t + 1] = one / (d_ref[t : t + 1] + e_ref[t : t + 1] - diagonal(t))
    for k in range(2 * chips):
        fs, gs = f_ref[k * T : k * T + 1], g_ref[k * T : k * T + 1]
        for j in range(1, T):
            fs = fs * f_ref[k * T + j : k * T + j + 1]
            gs = gs * g_ref[k * T + j : k * T + j + 1]
        a_ref[k : k + 1] = fs
        c_ref[k : k + 1] = gs
    k = lax.axis_index("tm")
    z = k // 2
    for j in range(T):
        out_ref[j : j + 1] = f_ref[pl.ds(k * T + j, 1)]
        out_ref[T + j : T + j + 1] = g_ref[pl.ds(k * T + j, 1)]
        out_ref[2 * T + j : 2 * T + j + 1] = d_ref[pl.ds(k * T + j, 1)]
    out_ref[12:13] = a_ref[pl.ds(2 * z + 1, 1)]
    out_ref[13:14] = c_ref[pl.ds(2 * z, 1)]
    out_ref[14:15] = a_ref[pl.ds(2 * z, 1)]
    out_ref[15:16] = c_ref[pl.ds(2 * z + 1, 1)]
    forward, backward = one, one
    earliest, latest = {}, {}
    for d in range(1, chips):
        earliest[d], latest[d] = forward, backward
        before = jnp.maximum(z - d, 0)
        after = jnp.minimum(z + d, chips - 1)
        forward = forward * a_ref[pl.ds(2 * before, 1)] * a_ref[pl.ds(2 * before + 1, 1)]
        backward = backward * c_ref[pl.ds(2 * after, 1)] * c_ref[pl.ds(2 * after + 1, 1)]
    ahead = k % 2 == 0
    for d in range(1, HALF + 1):
        whole = chips - d
        is_forward = jnp.where(jnp.logical_or(ahead, d == HALF), z >= d, z + d >= chips)
        weight = jnp.where(
            jnp.logical_or(ahead, d == HALF),
            jnp.where(is_forward, earliest[d], latest[whole]),
            jnp.where(is_forward, earliest[whole], latest[d]),
        )
        out_ref[15 + d : 16 + d] = jnp.where(is_forward, weight, zero)
        out_ref[19 + d : 20 + d] = jnp.where(is_forward, zero, weight)


def coefficients(gaps):
    years = gaps.shape[0]
    return pl.pallas_call(
        coefficient_kernel,
        in_specs=[pl.BlockSpec(memory_space=pltpu.SMEM)],
        out_specs=vmem(),
        out_shape=sds((24, B), F32),
        scratch_shapes=[pltpu.VMEM((years, B), F32)] * 5 + [pltpu.VMEM((16, B), F32)] * 2,
        compiler_params=PARAMS(),
        cost_estimate=cost(years * B * 200, years * 600),
        name="coefficients",
    )(gaps)


def gradient_kernel(first, *refs):
    n, c, extra = refs[:Q], refs[Q : 2 * Q], refs[2 * Q]
    refs = refs[2 * Q + 1 :]
    if first:
        words = [[word_block(n[i], t) for i in range(Q)] for t in range(T)]
    else:
        words = [[r[t] for r in refs[:Q]] for t in range(T)]
        refs = refs[Q:]
    gw, gc, coeff_ref = refs[:Q], refs[Q : 2 * Q], refs[2 * Q]
    vocab = Q * Q * B
    for t in range(T):
        panel = jnp.concatenate([r[t] for r in c], 1)
        for i in range(Q):
            block = words[t][i].astype(F32).T
            negative = (block[:, E : E + 1] + block[:, E + 1 : E + 2]) * (1.0 / vocab)
            scores = jnp.dot(block.astype(BF16), panel, preferred_element_type=F32)
            sig = 1.0 / (1.0 + jnp.exp(-scores))
            weights = jnp.concatenate([count_block(n[i], t, j) for j in range(Q)], 1).astype(F32)
            coeff_ref[t % 2, i * B : (i + 1) * B, :] = (
                weights * (1.0 - sig) - negative * sig
            ).astype(BF16)
        coeff = coeff_ref[t % 2]
        word_grad = lax.dot_general(
            panel, coeff, (((1,), (1,)), ((), ())), preferred_element_type=F32
        )
        ctx_grad = jnp.dot(
            jnp.concatenate(words[t], 1), coeff, preferred_element_type=F32
        ).astype(BF16)
        if not first:
            word_grad = jnp.concatenate([word_grad[:E], extra[t]], 0)
        word_grad = word_grad.astype(BF16)
        for i in range(Q):
            gw[i][t] = word_grad[:, i * B : (i + 1) * B]
            gc[i][t] = ctx_grad[:, i * B : (i + 1) * B]
    if first:
        for i in range(Q):
            gw[i][T] = extra[0]
            gc[i][T] = extra[1]


def gradients(n, c, extra, w=()):
    first = not w
    return pl.pallas_call(
        functools.partial(gradient_kernel, first),
        in_specs=[vmem()] * (2 * Q + 1 + len(w)),
        out_specs=[vmem()] * (2 * Q),
        out_shape=[sds((T + first, EP, B), BF16)] * (2 * Q),
        scratch_shapes=[pltpu.VMEM((2, Q * B, Q * B), BF16)],
        compiler_params=PARAMS(),
        cost_estimate=cost(6 * T * 512 * 512 * EP, 6 << 20, 2 * T * 512 * 512),
        name="gradients",
    )(*n, *c, extra, *w)


def entropy(scores):
    size = jnp.abs(scores)
    small = jnp.exp(-size)
    upper = 1.0 / (1.0 + small)
    lower = small * upper
    return jnp.where(scores >= 0, upper, lower), jnp.log(upper) - lower * size


def drift_kernel(*refs):
    n, c, gw, gc = (refs[i * Q : (i + 1) * Q] for i in range(4))
    out_ref, p_ref, h_ref = refs[4 * Q :]
    tiny = jnp.finfo(F32).tiny
    row = lax.broadcasted_iota(jnp.int32, (8, B), 0)
    for i in range(Q):
        for t in range(T + 1):
            if t < T:
                panel = jnp.concatenate([r[t] for r in c], 1)
                block = word_block(n[i], t)
            else:
                panel = jnp.concatenate([gc[-j % Q][T] for j in range(Q)], 1)
                block = gw[-i % Q][T]
            scores = jnp.dot(block.astype(F32).T.astype(BF16), panel, preferred_element_type=F32)
            p, h = entropy(scores)
            if t > 0:
                m = 0.5 * (p_ref[...] + p)
                rest = 1.0 - m
                mixed = m * jnp.log(jnp.maximum(m, tiny)) + rest * jnp.log(jnp.maximum(rest, tiny))
                js = 0.5 * (h_ref[...] + h) - mixed
                total = js[:, :B] + js[:, B : 2 * B] + js[:, 2 * B : 3 * B] + js[:, 3 * B :]
                total = jnp.sum(total.T, axis=0, keepdims=True)
                high = total.astype(BF16).astype(F32)
                out_ref[t - 1, :, i * B : (i + 1) * B] = jnp.where(
                    row == 0, high, jnp.where(row == 1, total - high, 0.0)
                )
            if t < T:
                p_ref[...] = p
                h_ref[...] = h


def drift_parts(n, c, gw, gc):
    return pl.pallas_call(
        drift_kernel,
        in_specs=[vmem()] * (4 * Q),
        out_specs=vmem(),
        out_shape=sds((T, 8, Q * B), F32),
        scratch_shapes=[pltpu.VMEM((B, Q * B), F32)] * 2,
        compiler_params=PARAMS(),
        cost_estimate=cost(2 * 5 * 512 * 512 * (EP + 30), 4 << 20, 5 * 5 * 512 * 512),
        name="drift",
    )(*n, *c, *gw, *gc)


def summary_kernel(*refs):
    parts = (refs[0:Q], refs[Q : 2 * Q])
    co_ref, b_ref, own_ref = refs[2 * Q :]
    for q in range(2):
        for t in range(T):
            total = parts[q][0][t].astype(F32)
            for r in parts[q][1:]:
                total = total + r[t].astype(F32)
            b_ref[q, t] = total
        forward = b_ref[q, 0]
        for t in range(1, T):
            forward = b_ref[q, t] + co_ref[t : t + 1] * forward
        backward = b_ref[q, T - 1]
        for t in reversed(range(T - 1)):
            backward = b_ref[q, t] + co_ref[T + t : T + t + 1] * backward
        own_ref[q] = forward
        own_ref[2 + q] = backward


def summaries(gw, gc, co):
    return pl.pallas_call(
        summary_kernel,
        in_specs=[vmem()] * (2 * Q + 1),
        out_specs=[vmem()] * 2,
        out_shape=[sds((2, T, EP, B), F32), sds((4, EP, B), F32)],
        compiler_params=PARAMS(),
        cost_estimate=cost(2 * T * EP * B * 10, 3 << 20),
        name="summaries",
    )(*gw, *gc, co)


def chip_kernel(own_ref, other_ref, co_ref, *outs):
    k = lax.axis_index("tm")
    even, z = k % 2 == 0, k // 2
    chips = 2 * HALF
    for q in range(2):
        own, other = own_ref[q], other_ref[q]
        forward = jnp.where(even, other, own) + co_ref[12:13] * jnp.where(even, own, other)
        own, other = own_ref[2 + q], other_ref[2 + q]
        backward = jnp.where(even, own, other) + co_ref[13:14] * jnp.where(even, other, own)
        for d in range(1, HALF):
            is_forward = jnp.where(even, z + d < chips, z < d)
            outs[d - 1][q] = jnp.where(is_forward, forward, backward).astype(BF16)

        @pl.when(k % 2 == q)
        def _():
            outs[HALF - 1][...] = jnp.where(z < HALF, forward, backward).astype(BF16)


def chip_summaries(own, other, co):
    return pl.pallas_call(
        chip_kernel,
        in_specs=[vmem()] * 3,
        out_specs=[vmem()] * HALF,
        out_shape=[sds((2, EP, B), BF16)] * (HALF - 1) + [sds((EP, B), BF16)],
        compiler_params=PARAMS(),
        cost_estimate=cost(EP * B * 16, 1 << 20),
        name="chip_summaries",
    )(own, other, co)


def incoming_kernel(*refs):
    got, co_ref, out_ref = refs[:HALF], refs[HALF], refs[HALF + 1]
    core = lax.axis_index("tm") % 2
    for q in range(2):
        for way in range(2):
            row = 16 + 4 * way
            total = co_ref[row : row + 1] * got[0][q].astype(F32)
            for d in range(2, HALF):
                total = total + co_ref[row + d - 1 : row + d] * got[d - 1][q].astype(F32)
            across = co_ref[row + HALF - 1 : row + HALF] * got[HALF - 1][...].astype(F32)
            out_ref[2 * way + q] = total + jnp.where(core == q, across, jnp.zeros_like(across))


def incoming(got, co):
    return pl.pallas_call(
        incoming_kernel,
        in_specs=[vmem()] * (HALF + 1),
        out_specs=vmem(),
        out_shape=sds((4, EP, B), F32),
        compiler_params=PARAMS(),
        cost_estimate=cost(4 * EP * B * 8, 1 << 20),
        name="incoming",
    )(*got, co)


def entering(odd, q, near_ref, mine_ref, other_ref, co_ref):
    y = mine_ref[q] + other_ref[q]
    z = mine_ref[2 + q] + other_ref[2 + q]
    y_odd = near_ref[q] + co_ref[14:15] * y
    z_even = near_ref[2 + q] + co_ref[15:16] * z
    return jnp.where(odd, y_odd, y), jnp.where(odd, z, z_even)


def solved_years(b_ref, q, y, z, co_ref):
    ys = []
    for t in range(T):
        y = b_ref[q, t] + co_ref[t : t + 1] * y
        ys.append(y)
    out = [None] * T
    for t in reversed(range(T)):
        carried = co_ref[T + t : T + t + 1] * z
        z = b_ref[q, t] + carried
        out[t] = (ys[t] + carried) * co_ref[2 * T + t : 2 * T + t + 1]
    return out


def update_kernel(scale, b_ref, near_ref, mine_ref, other_ref, co_ref, w_ref, c_ref, nw_ref, nc_ref):
    odd = lax.axis_index("tm") % 2 == 1
    live = lax.broadcasted_iota(jnp.int32, (EP, B), 0) < E
    for q, (old, new) in enumerate(((w_ref, nw_ref), (c_ref, nc_ref))):
        y, z = entering(odd, q, near_ref, mine_ref, other_ref, co_ref)
        solved = solved_years(b_ref, q, y, z, co_ref)
        for t in range(T):
            before = word_block(old, t) if q == 0 else old[t]
            new[t] = (before.astype(F32) + jnp.where(live, scale * solved[t], 0.0)).astype(BF16)


def finish_kernel(
    scale, vocab, b_ref, near_ref, mine_ref, other_ref, co_ref, w_ref, c_ref, nw_ref, nc_ref, dr_ref
):
    k = lax.axis_index("tm")
    odd, last = k % 2 == 1, k == lax.axis_size("tm") - 1
    for q, (old, new) in enumerate(((w_ref, nw_ref), (c_ref, nc_ref))):
        y, z = entering(odd, q, near_ref, mine_ref, other_ref, co_ref)
        solved = solved_years(b_ref, q, y, z, co_ref)
        for t in range(T):
            fresh = old[t].astype(F32) + scale * solved[t]
            new[t] = fresh[:E].astype(BF16)
    for t in range(T):
        total = (b_ref[0, t, E : E + 1] + b_ref[0, t, E + 1 : E + 2]) * (float(vocab) ** -0.5)
        if t == T - 1:
            total = jnp.where(last, jnp.zeros_like(total), total)
        dr_ref[t : t + 1] = total


def update(scale, b, near, mine, other, co, words, contexts):
    return pl.pallas_call(
        functools.partial(update_kernel, scale),
        in_specs=[vmem()] * 7,
        out_specs=[vmem()] * 2,
        out_shape=[sds((T, EP, B), BF16)] * 2,
        compiler_params=PARAMS(),
        cost_estimate=cost(2 * T * EP * B * 10, 3 << 20),
        name="update",
    )(b, near, mine, other, co, words, contexts)


def finish(scale, vocab, b, near, mine, other, co, words, contexts):
    return pl.pallas_call(
        functools.partial(finish_kernel, scale, vocab),
        in_specs=[vmem()] * 7,
        out_specs=[vmem()] * 3,
        out_shape=[sds((T, E, B), BF16)] * 2 + [sds((T, B), F32)],
        compiler_params=PARAMS(),
        cost_estimate=cost(2 * T * EP * B * 10, 3 << 20),
        name="finish",
    )(b, near, mine, other, co, words, contexts)


def step(v, s, rows):
    y, x = v // Q, v % Q
    return y * Q + (x + s) % Q if rows else ((y + s) % Q) * Q + x


def in_grid(a, s, of_words):
    years, places = lax.axis_size("tm"), Q * Q
    pairs = [
        (k * places + v, k * places + step(v, s, (k % 2 == 0) == of_words))
        for k in range(years)
        for v in range(places)
    ]
    return lax.ppermute(a, ("tm", "vocab"), pairs)


def other_core(a):
    return lax.ppermute(a, "tm", [(k, k ^ 1) for k in range(lax.axis_size("tm"))])


def along_z(a, d):
    chips = lax.axis_size("tm") // 2
    ahead = [(2 * z, 2 * ((z + d) % chips)) for z in range(chips)]
    back = [(2 * z + 1, 2 * ((z - d) % chips) + 1) for z in range(chips)]
    return lax.ppermute(a, "tm", ahead + back)


def from_next(a):
    return lax.ppermute(a, "tm", [(k, k - 1) for k in range(1, lax.axis_size("tm"))])


ORDER = (2, 1, 3)


def spread(parts, of_words):
    got = {s: in_grid(parts[s], s, of_words) for s in ORDER}
    return [parts[0]] + [got[s] for s in range(1, Q)]


def collected(parts, of_words):
    got = {s: in_grid(parts[s], -s, of_words) for s in ORDER}
    return [parts[0]] + [got[s] for s in range(1, Q)]


def on_device(counts, word_vecs, ctx_vecs, gaps):
    vocab = counts.shape[2]
    scale = RATE / float(vocab) ** 0.5
    *loads, contexts, first = stage(
        counts, word_vecs.transpose(0, 2, 1), ctx_vecs.transpose(0, 2, 1)
    )
    words = loads[0]
    n, c = spread(loads, True), spread([contexts] * Q, False)
    following = from_next(first)
    co = coefficients(gaps)
    w, extra = (), following
    for sweep in range(SWEEPS):
        last = sweep == SWEEPS - 1
        if sweep:
            w, c = spread([words] * Q, True), spread([contexts] * Q, False)
        grads = gradients(n, c, extra, w)
        gw, gc = collected(grads[:Q], True), collected(grads[Q:], False)
        b, own = summaries(gw, gc, co)
        near = other_core(own)
        outs = chip_summaries(own, near, co)
        if sweep == 0:
            outs, held = lax.optimization_barrier((outs, c))
            extra = drift_parts(n, held, gw, gc)
        got = {d: along_z(outs[d - 1], d) for d in (4, 3, 2, 1)}
        got = [got[d] for d in range(1, HALF + 1)]
        if sweep == 0:
            got, extra = lax.optimization_barrier((got, extra))
        mine = incoming(got, co)
        other = other_core(mine)
        if last:
            words, contexts, drift = finish(scale, vocab, b, near, mine, other, co, words, contexts)
            return (words.transpose(0, 2, 1), contexts.transpose(0, 2, 1), drift)
        words, contexts = update(scale, b, near, mine, other, co, words, contexts)


def solution(mesh):
    return jax.shard_map(
        on_device,
        mesh=mesh,
        in_specs=(P("tm", "vocab", None), P("tm", "vocab", None), P("tm", "vocab", None), P()),
        out_specs=(P("tm", "vocab", None), P("tm", "vocab", None), P("tm", "vocab")),
        check_vma=False,
    )
```

```python
import functools

import jax
import jax.numpy as jnp
from jax import lax
from jax.experimental import pallas as pl
from jax.experimental.pallas import tpu as pltpu
from jax.sharding import PartitionSpec as P

PRIOR = 0.05
DIFF = 0.5
RATE = 0.2
SWEEPS = 2


E = 200
EP = 208
B = 128
T = 4
Q = 4
HALF = 4
F32 = jnp.float32
BF16 = jnp.bfloat16

PARAMS = functools.partial(pltpu.CompilerParams, vmem_limit_bytes=24 * 1024 * 1024)


def sds(shape, dtype):
    return jax.ShapeDtypeStruct(shape, dtype)


def vmem():
    return pl.BlockSpec(memory_space=pltpu.VMEM)


def cost(flops, moved, special=0):
    return pl.CostEstimate(flops=int(flops), bytes_accessed=int(moved), transcendentals=int(special))


COUNT_ROWS = T * Q * B
ROWS = COUNT_ROWS + T * EP


def count_block(ref, t, j):
    at = (t * Q + j) * B
    return ref[at : at + B]


def word_block(ref, t):
    at = COUNT_ROWS + t * EP
    return ref[at : at + EP]


def stage_kernel(counts_ref, w_ref, *loads):
    along_rows = lax.axis_index("tm") % 2 == 0
    place = lax.axis_index("vocab")
    y, x = place // Q, place % Q
    row = lax.broadcasted_iota(jnp.int32, (8, B), 0)
    ones = jnp.ones((8, B), BF16)
    for t in range(T):
        total = jnp.zeros((8, B), F32)
        for s in range(Q):
            for j in range(Q):
                block = jnp.where(
                    along_rows,
                    ((y + Q - j) % Q) * Q + (x + s) % Q,
                    ((y + s) % Q) * Q + (x + Q - j) % Q,
                )
                at = pl.multiple_of(block * B, B)
                to = (t * Q + j) * B
                part = counts_ref[t, :, pl.ds(at, B)].astype(F32).astype(BF16)
                loads[s][to : to + B] = part
                total = total + lax.dot_general(
                    ones, part, (((1,), (1,)), ((), ())), preferred_element_type=F32
                )
        high = total.astype(BF16).astype(F32)
        spare = jnp.where(row == 0, high, jnp.where(row == 1, total - high, 0.0))
        word = jnp.concatenate([w_ref[t].astype(F32), spare], 0).astype(BF16)
        for s in range(Q):
            loads[s][COUNT_ROWS + t * EP : COUNT_ROWS + (t + 1) * EP] = word


def stage(counts, words):
    vocab = counts.shape[2]
    return pl.pallas_call(
        stage_kernel,
        in_specs=[vmem()] * 2,
        out_specs=[vmem()] * Q,
        out_shape=[sds((ROWS, B), BF16)] * Q,
        compiler_params=PARAMS(),
        cost_estimate=cost(T * B * vocab * 16, T * B * vocab * 6),
        name="stage",
    )(counts, words)


def coefficient_kernel(gaps_ref, out_ref, link_ref, f_ref, g_ref, d_ref, e_ref, a_ref, c_ref):
    years = gaps_ref.shape[0]
    chips = years // (2 * T)
    one = jnp.ones((1, B), F32)
    zero = jnp.zeros((1, B), F32)
    for t in range(years - 1):
        link_ref[t : t + 1] = one / (DIFF * (one * gaps_ref[t].astype(F32)))

    def link(t):
        return link_ref[t : t + 1] if 0 <= t < years - 1 else zero

    def diagonal(t):
        return PRIOR + link(t - 1) + link(t)

    delta, eps = diagonal(0), diagonal(years - 1)
    f_ref[0:1] = zero
    g_ref[years - 1 : years] = zero
    d_ref[0:1] = delta
    e_ref[years - 1 : years] = eps
    for t in range(1, years):
        f = link(t - 1) / delta
        delta = diagonal(t) - link(t - 1) * f
        f_ref[t : t + 1] = f
        d_ref[t : t + 1] = delta
        u = years - 1 - t
        g = link(u) / eps
        eps = diagonal(u) - link(u) * g
        g_ref[u : u + 1] = g
        e_ref[u : u + 1] = eps
    for t in range(years):
        d_ref[t : t + 1] = one / (d_ref[t : t + 1] + e_ref[t : t + 1] - diagonal(t))
    for k in range(2 * chips):
        fs, gs = f_ref[k * T : k * T + 1], g_ref[k * T : k * T + 1]
        for j in range(1, T):
            fs = fs * f_ref[k * T + j : k * T + j + 1]
            gs = gs * g_ref[k * T + j : k * T + j + 1]
        a_ref[k : k + 1] = fs
        c_ref[k : k + 1] = gs
    k = lax.axis_index("tm")
    z = k // 2
    for j in range(T):
        out_ref[j : j + 1] = f_ref[pl.ds(k * T + j, 1)]
        out_ref[T + j : T + j + 1] = g_ref[pl.ds(k * T + j, 1)]
        out_ref[2 * T + j : 2 * T + j + 1] = d_ref[pl.ds(k * T + j, 1)]
    out_ref[12:13] = a_ref[pl.ds(2 * z + 1, 1)]
    out_ref[13:14] = c_ref[pl.ds(2 * z, 1)]
    out_ref[14:15] = a_ref[pl.ds(2 * z, 1)]
    out_ref[15:16] = c_ref[pl.ds(2 * z + 1, 1)]
    forward, backward = one, one
    earliest, latest = {}, {}
    for d in range(1, chips):
        earliest[d], latest[d] = forward, backward
        before = jnp.maximum(z - d, 0)
        after = jnp.minimum(z + d, chips - 1)
        forward = forward * a_ref[pl.ds(2 * before, 1)] * a_ref[pl.ds(2 * before + 1, 1)]
        backward = backward * c_ref[pl.ds(2 * after, 1)] * c_ref[pl.ds(2 * after + 1, 1)]
    ahead = k % 2 == 0
    for d in range(1, HALF + 1):
        whole = chips - d
        is_forward = jnp.where(jnp.logical_or(ahead, d == HALF), z >= d, z + d >= chips)
        weight = jnp.where(
            jnp.logical_or(ahead, d == HALF),
            jnp.where(is_forward, earliest[d], latest[whole]),
            jnp.where(is_forward, earliest[whole], latest[d]),
        )
        out_ref[15 + d : 16 + d] = jnp.where(is_forward, weight, zero)
        out_ref[19 + d : 20 + d] = jnp.where(is_forward, zero, weight)


def coefficients(gaps):
    years = gaps.shape[0]
    return pl.pallas_call(
        coefficient_kernel,
        in_specs=[pl.BlockSpec(memory_space=pltpu.SMEM)],
        out_specs=vmem(),
        out_shape=sds((24, B), F32),
        scratch_shapes=[pltpu.VMEM((years, B), F32)] * 5 + [pltpu.VMEM((16, B), F32)] * 2,
        compiler_params=PARAMS(),
        cost_estimate=cost(years * B * 200, years * 600),
        name="coefficients",
    )(gaps)


def gradient_kernel(first, *refs):
    n, c, extra = refs[:Q], refs[Q : 2 * Q], refs[2 * Q]
    refs = refs[2 * Q + 1 :]
    if not first:
        w, refs = refs[:Q], refs[Q:]
    gw, gc, coeff_ref = refs[:Q], refs[Q : 2 * Q], refs[2 * Q]
    vocab = Q * Q * B
    for t in range(T):
        panel = jnp.concatenate([r[t] for r in c], 1)
        words = []
        for i in range(Q):
            loaded = word_block(n[i], t).astype(F32)
            block = loaded[:E] if first else w[i][t].astype(F32)
            words.append(block.astype(BF16))
            spare = loaded[E:].T
            negative = (spare[:, 0:1] + spare[:, 1:2]) * (1.0 / vocab)
            scores = jnp.dot(block.T.astype(BF16), panel, preferred_element_type=F32)
            weights = jnp.concatenate([count_block(n[i], t, j) for j in range(Q)], 1).astype(F32)
            half = jnp.tanh(0.5 * scores)
            coeff = 0.5 * ((weights - negative) - (weights + negative) * half)
            coeff_ref[t % 2, i * B : (i + 1) * B, :] = coeff.astype(BF16)
        coeff = coeff_ref[t % 2]
        word_grad = lax.dot_general(
            panel, coeff, (((1,), (1,)), ((), ())), preferred_element_type=F32
        )
        ctx_grad = jnp.dot(
            jnp.concatenate(words, 1), coeff, preferred_element_type=F32
        ).astype(BF16)
        if not first:
            word_grad = jnp.concatenate([word_grad, extra[t]], 0)
        word_grad = word_grad.astype(BF16)
        for i in range(Q):
            gw[i][t] = word_grad[:, i * B : (i + 1) * B]
            gc[i][t] = ctx_grad[:, i * B : (i + 1) * B]
    if first:
        for i in range(Q):
            gw[i][T] = extra[0]
            gc[i][T] = extra[1]


def gradients(n, c, extra, w=()):
    first = not w
    return pl.pallas_call(
        functools.partial(gradient_kernel, first),
        in_specs=[vmem()] * (2 * Q + 1 + len(w)),
        out_specs=[vmem()] * (2 * Q),
        out_shape=[sds((T + first, E if first else EP, B), BF16)] * Q
        + [sds((T + first, E, B), BF16)] * Q,
        scratch_shapes=[pltpu.VMEM((2, Q * B, Q * B), BF16)],
        compiler_params=PARAMS(),
        cost_estimate=cost(6 * T * 512 * 512 * EP, 6 << 20, 2 * T * 512 * 512),
        name="gradients",
    )(*n, *c, extra, *w)


def entropy(scores):
    size = jnp.abs(scores)
    small = jnp.exp(-size)
    upper = 1.0 / (1.0 + small)
    lower = small * upper
    return jnp.where(scores >= 0, upper, lower), jnp.log(upper) - lower * size


def drift_kernel(*refs):
    n, c, gw, gc = (refs[i * Q : (i + 1) * Q] for i in range(4))
    out_ref, p_ref, h_ref = refs[4 * Q :]
    tiny = jnp.finfo(F32).tiny
    row = lax.broadcasted_iota(jnp.int32, (8, B), 0)
    for i in range(Q):
        for t in range(T + 1):
            if t < T:
                panel = jnp.concatenate([r[t] for r in c], 1)
                block = word_block(n[i], t).astype(F32)[:E]
            else:
                panel = jnp.concatenate([gc[-j % Q][T] for j in range(Q)], 1)
                block = gw[-i % Q][T].astype(F32)
            scores = jnp.dot(block.T.astype(BF16), panel, preferred_element_type=F32)
            p, h = entropy(scores)
            if t > 0:
                m = 0.5 * (p_ref[...] + p)
                rest = 1.0 - m
                mixed = m * jnp.log(jnp.maximum(m, tiny)) + rest * jnp.log(jnp.maximum(rest, tiny))
                js = 0.5 * (h_ref[...] + h) - mixed
                total = js[:, :B] + js[:, B : 2 * B] + js[:, 2 * B : 3 * B] + js[:, 3 * B :]
                total = jnp.sum(total.T, axis=0, keepdims=True)
                high = total.astype(BF16).astype(F32)
                out_ref[t - 1, :, i * B : (i + 1) * B] = jnp.where(
                    row == 0, high, jnp.where(row == 1, total - high, 0.0)
                )
            if t < T:
                p_ref[...] = p
                h_ref[...] = h


def drift_parts(n, c, gw, gc):
    return pl.pallas_call(
        drift_kernel,
        in_specs=[vmem()] * (4 * Q),
        out_specs=vmem(),
        out_shape=sds((T, 8, Q * B), F32),
        scratch_shapes=[pltpu.VMEM((B, Q * B), F32)] * 2,
        compiler_params=PARAMS(),
        cost_estimate=cost(2 * 5 * 512 * 512 * (EP + 30), 4 << 20, 5 * 5 * 512 * 512),
        name="drift",
    )(*n, *c, *gw, *gc)


def summary_kernel(drift, *refs):
    parts = (refs[0:Q], refs[Q : 2 * Q])
    co_ref, b_ref, own_ref = refs[2 * Q : 2 * Q + 3]
    for q in range(2):
        for t in range(T):
            total = parts[q][0][t].astype(F32)
            for r in parts[q][1:]:
                total = total + r[t].astype(F32)
            if drift and q == 0:
                spare, total = total[E:], total[:E]
                refs[-1][t : t + 1] = spare[0:1] + spare[1:2]
            b_ref[q, t] = total
        forward = b_ref[q, 0]
        for t in range(1, T):
            forward = b_ref[q, t] + co_ref[t : t + 1] * forward
        backward = b_ref[q, T - 1]
        for t in reversed(range(T - 1)):
            backward = b_ref[q, t] + co_ref[T + t : T + t + 1] * backward
        own_ref[q] = forward.astype(BF16)
        own_ref[2 + q] = backward.astype(BF16)


def summaries(gw, gc, co, drift):
    return pl.pallas_call(
        functools.partial(summary_kernel, drift),
        in_specs=[vmem()] * (2 * Q + 1),
        out_specs=[vmem()] * (2 + drift),
        out_shape=[sds((2, T, E, B), F32), sds((4, E, B), BF16)] + [sds((T, B), F32)] * drift,
        compiler_params=PARAMS(),
        cost_estimate=cost(2 * T * EP * B * 10, 3 << 20),
        name="summaries",
    )(*gw, *gc, co)


def chip_kernel(own_ref, other_ref, co_ref, *outs):
    k = lax.axis_index("tm")
    even, z = k % 2 == 0, k // 2
    chips = 2 * HALF
    for q in range(2):
        own, other = own_ref[q].astype(F32), other_ref[q].astype(F32)
        forward = jnp.where(even, other, own) + co_ref[12:13] * jnp.where(even, own, other)
        own, other = own_ref[2 + q].astype(F32), other_ref[2 + q].astype(F32)
        backward = jnp.where(even, own, other) + co_ref[13:14] * jnp.where(even, other, own)
        for d in range(1, HALF):
            is_forward = jnp.where(even, z + d < chips, z < d)
            outs[d - 1][q] = jnp.where(is_forward, forward, backward).astype(BF16)

        @pl.when(k % 2 == q)
        def _():
            outs[HALF - 1][...] = jnp.where(z < HALF, forward, backward).astype(BF16)


def chip_summaries(own, other, co):
    return pl.pallas_call(
        chip_kernel,
        in_specs=[vmem()] * 3,
        out_specs=[vmem()] * HALF,
        out_shape=[sds((2, E, B), BF16)] * (HALF - 1) + [sds((E, B), BF16)],
        compiler_params=PARAMS(),
        cost_estimate=cost(EP * B * 16, 1 << 20),
        name="chip_summaries",
    )(own, other, co)


def incoming_kernel(*refs):
    got, co_ref, out_ref = refs[:HALF], refs[HALF], refs[HALF + 1]
    core = lax.axis_index("tm") % 2
    for q in range(2):
        for way in range(2):
            row = 16 + 4 * way
            total = co_ref[row : row + 1] * got[0][q].astype(F32)
            for d in range(2, HALF):
                total = total + co_ref[row + d - 1 : row + d] * got[d - 1][q].astype(F32)
            across = co_ref[row + HALF - 1 : row + HALF] * got[HALF - 1][...].astype(F32)
            total = total + jnp.where(core == q, across, jnp.zeros_like(across))
            out_ref[2 * way + q] = total.astype(BF16)


def incoming(got, co):
    return pl.pallas_call(
        incoming_kernel,
        in_specs=[vmem()] * (HALF + 1),
        out_specs=vmem(),
        out_shape=sds((4, E, B), BF16),
        compiler_params=PARAMS(),
        cost_estimate=cost(4 * EP * B * 8, 1 << 20),
        name="incoming",
    )(*got, co)


def entering(odd, q, near_ref, mine_ref, other_ref, co_ref):
    y = mine_ref[q].astype(F32) + other_ref[q].astype(F32)
    z = mine_ref[2 + q].astype(F32) + other_ref[2 + q].astype(F32)
    y_odd = near_ref[q].astype(F32) + co_ref[14:15] * y
    z_even = near_ref[2 + q].astype(F32) + co_ref[15:16] * z
    return jnp.where(odd, y_odd, y), jnp.where(odd, z, z_even)


def solved_years(b_ref, q, y, z, co_ref):
    ys = []
    for t in range(T):
        y = b_ref[q, t] + co_ref[t : t + 1] * y
        ys.append(y)
    out = [None] * T
    for t in reversed(range(T)):
        carried = co_ref[T + t : T + t + 1] * z
        z = b_ref[q, t] + carried
        out[t] = (ys[t] + carried) * co_ref[2 * T + t : 2 * T + t + 1]
    return out


def update_kernel(scale, b_ref, near_ref, mine_ref, other_ref, co_ref, w_ref, c_ref, *refs):
    odd = lax.axis_index("tm") % 2 == 1
    for q, (old, new) in enumerate(((w_ref, refs[-2]), (c_ref, refs[-1]))):
        y, z = entering(odd, q, near_ref, mine_ref, other_ref, co_ref)
        solved = solved_years(b_ref, q, y, z, co_ref)
        for t in range(T):
            new[t] = (old[t].astype(F32) + scale * solved[t]).astype(BF16)


def finish_kernel(scale, vocab, *refs):
    *ins, raw_ref, nw_ref, nc_ref, drift_ref = refs
    update_kernel(scale, *ins, nw_ref, nc_ref)
    last = lax.axis_index("tm") == lax.axis_size("tm") - 1
    drift = raw_ref[...] * (float(vocab) ** -0.5)
    at = lax.broadcasted_iota(jnp.int32, (T, B), 0)
    drift_ref[...] = jnp.where(jnp.logical_and(last, at == T - 1), 0.0, drift)


def update(scale, *arrays):
    return pl.pallas_call(
        functools.partial(update_kernel, scale),
        in_specs=[vmem()] * 7,
        out_specs=[vmem()] * 2,
        out_shape=[sds((T, E, B), BF16)] * 2,
        compiler_params=PARAMS(),
        cost_estimate=cost(2 * T * EP * B * 10, 3 << 20),
        name="update",
    )(*arrays)


def finish(scale, vocab, *arrays):
    return pl.pallas_call(
        functools.partial(finish_kernel, scale, vocab),
        in_specs=[vmem()] * 8,
        out_specs=[vmem()] * 3,
        out_shape=[sds((T, E, B), BF16)] * 2 + [sds((T, B), F32)],
        compiler_params=PARAMS(),
        cost_estimate=cost(2 * T * EP * B * 10, 3 << 20),
        name="finish",
    )(*arrays)


def step(v, s, rows):
    y, x = v // Q, v % Q
    return y * Q + (x + s) % Q if rows else ((y + s) % Q) * Q + x


def in_grid(a, s, of_words):
    years, places = lax.axis_size("tm"), Q * Q
    pairs = [
        (k * places + v, k * places + step(v, s, (k % 2 == 0) == of_words))
        for k in range(years)
        for v in range(places)
    ]
    return lax.ppermute(a, ("tm", "vocab"), pairs)


def other_core(a):
    return lax.ppermute(a, "tm", [(k, k ^ 1) for k in range(lax.axis_size("tm"))])


def along_z(a, d):
    chips = lax.axis_size("tm") // 2
    ahead = [(2 * z, 2 * ((z + d) % chips)) for z in range(chips)]
    back = [(2 * z + 1, 2 * ((z - d) % chips) + 1) for z in range(chips)]
    return lax.ppermute(a, "tm", ahead + back)


def from_next(a):
    return lax.ppermute(a, "tm", [(k, k - 1) for k in range(1, lax.axis_size("tm"))])


ORDER = (1, 2, 3)


def spread(words, contexts):
    w, c = {0: words[0]}, {0: contexts[0]}
    for s in ORDER:
        w[s] = in_grid(words[s], s, True)
        c[s] = in_grid(contexts[s], s, False)
    return [w[s] for s in range(Q)], [c[s] for s in range(Q)]


def collected(words, contexts):
    w, c = {0: words[0]}, {0: contexts[0]}
    for s in ORDER:
        w[s] = in_grid(words[s], -s, True)
        c[s] = in_grid(contexts[s], -s, False)
    return [w[s] for s in range(Q)], [c[s] for s in range(Q)]


def on_device(counts, word_vecs, ctx_vecs, gaps):
    vocab = counts.shape[2]
    scale = RATE / float(vocab) ** 0.5
    words, contexts = word_vecs.transpose(0, 2, 1), ctx_vecs.transpose(0, 2, 1)
    loads = stage(counts, words)
    n, c = spread(loads, [contexts] * Q)
    following = from_next(jnp.stack([words[0], contexts[0]], 0))
    co = coefficients(gaps)
    w, extra = (), following
    for sweep in range(SWEEPS):
        last = sweep == SWEEPS - 1
        if sweep:
            w, c = spread([words] * Q, [contexts] * Q)
        grads = gradients(n, c, extra, w)
        gw, gc = collected(grads[:Q], grads[Q:])
        b, own, *raw = summaries(gw, gc, co, last)
        near = other_core(own)
        outs = chip_summaries(own, near, co)
        if sweep == 0:
            outs, held = lax.optimization_barrier((outs, c))
            extra = drift_parts(n, held, gw, gc)
        got = {d: along_z(outs[d - 1], d) for d in (4, 3, 2, 1)}
        got = [got[d] for d in range(1, HALF + 1)]
        if sweep == 0:
            got, extra = lax.optimization_barrier((got, extra))
        mine = incoming(got, co)
        other = other_core(mine)
        if last:
            words, contexts, drift = finish(
                scale, vocab, b, near, mine, other, co, words, contexts, *raw
            )
            return (words.transpose(0, 2, 1), contexts.transpose(0, 2, 1), drift)
        words, contexts = update(scale, b, near, mine, other, co, words, contexts)


def solution(mesh):
    return jax.shard_map(
        on_device,
        mesh=mesh,
        in_specs=(P("tm", "vocab", None), P("tm", "vocab", None), P("tm", "vocab", None), P()),
        out_specs=(P("tm", "vocab", None), P("tm", "vocab", None), P("tm", "vocab")),
        check_vma=False,
    )
```

```python
import functools

import jax
import jax.numpy as jnp
from jax import lax
from jax.experimental import pallas as pl
from jax.experimental.pallas import tpu as pltpu
from jax.sharding import PartitionSpec as P

PRIOR = 0.05
DIFF = 0.5
RATE = 0.2
SWEEPS = 2


E = 200
EP = 208
B = 128
T = 4
Q = 4
HALF = 4
F32 = jnp.float32
BF16 = jnp.bfloat16

PARAMS = functools.partial(pltpu.CompilerParams, vmem_limit_bytes=24 * 1024 * 1024)


def sds(shape, dtype):
    return jax.ShapeDtypeStruct(shape, dtype)


def vmem():
    return pl.BlockSpec(memory_space=pltpu.VMEM)


def cost(flops, moved, special=0):
    return pl.CostEstimate(flops=int(flops), bytes_accessed=int(moved), transcendentals=int(special))


COUNT_ROWS = T * Q * B
ROWS = COUNT_ROWS + T * EP


def count_block(ref, t, j):
    at = (t * Q + j) * B
    return ref[at : at + B]


def word_block(ref, t):
    at = COUNT_ROWS + t * EP
    return ref[at : at + EP]


def stage_kernel(counts_ref, w_ref, *loads):
    along_rows = lax.axis_index("tm") % 2 == 0
    place = lax.axis_index("vocab")
    y, x = place // Q, place % Q
    row = lax.broadcasted_iota(jnp.int32, (8, B), 0)
    ones = jnp.ones((8, B), BF16)
    for t in range(T):
        total = jnp.zeros((8, B), F32)
        for s in range(Q):
            for j in range(Q):
                block = jnp.where(
                    along_rows,
                    ((y + Q - j) % Q) * Q + (x + s) % Q,
                    ((y + s) % Q) * Q + (x + Q - j) % Q,
                )
                at = pl.multiple_of(block * B, B)
                to = (t * Q + j) * B
                part = counts_ref[t, :, pl.ds(at, B)].astype(F32).astype(BF16)
                loads[s][to : to + B] = part
                total = total + lax.dot_general(
                    ones, part, (((1,), (1,)), ((), ())), preferred_element_type=F32
                )
        high = total.astype(BF16).astype(F32)
        spare = jnp.where(row == 0, high, jnp.where(row == 1, total - high, 0.0))
        word = jnp.concatenate([w_ref[t].astype(F32), spare], 0).astype(BF16)
        for s in range(Q):
            loads[s][COUNT_ROWS + t * EP : COUNT_ROWS + (t + 1) * EP] = word


def stage(counts, words):
    vocab = counts.shape[2]
    return pl.pallas_call(
        stage_kernel,
        in_specs=[vmem()] * 2,
        out_specs=[vmem()] * Q,
        out_shape=[sds((ROWS, B), BF16)] * Q,
        compiler_params=PARAMS(),
        cost_estimate=cost(T * B * vocab * 16, T * B * vocab * 6),
        name="stage",
    )(counts, words)


def coefficient_kernel(gaps_ref, out_ref, link_ref, f_ref, g_ref, d_ref, e_ref, a_ref, c_ref):
    years = gaps_ref.shape[0]
    chips = years // (2 * T)
    one = jnp.ones((1, B), F32)
    zero = jnp.zeros((1, B), F32)
    for t in range(years - 1):
        link_ref[t : t + 1] = one / (DIFF * (one * gaps_ref[t].astype(F32)))

    def link(t):
        return link_ref[t : t + 1] if 0 <= t < years - 1 else zero

    def diagonal(t):
        return PRIOR + link(t - 1) + link(t)

    delta, eps = diagonal(0), diagonal(years - 1)
    f_ref[0:1] = zero
    g_ref[years - 1 : years] = zero
    d_ref[0:1] = delta
    e_ref[years - 1 : years] = eps
    for t in range(1, years):
        f = link(t - 1) / delta
        delta = diagonal(t) - link(t - 1) * f
        f_ref[t : t + 1] = f
        d_ref[t : t + 1] = delta
        u = years - 1 - t
        g = link(u) / eps
        eps = diagonal(u) - link(u) * g
        g_ref[u : u + 1] = g
        e_ref[u : u + 1] = eps
    for t in range(years):
        d_ref[t : t + 1] = one / (d_ref[t : t + 1] + e_ref[t : t + 1] - diagonal(t))
    for k in range(2 * chips):
        fs, gs = f_ref[k * T : k * T + 1], g_ref[k * T : k * T + 1]
        for j in range(1, T):
            fs = fs * f_ref[k * T + j : k * T + j + 1]
            gs = gs * g_ref[k * T + j : k * T + j + 1]
        a_ref[k : k + 1] = fs
        c_ref[k : k + 1] = gs
    k = lax.axis_index("tm")
    z = k // 2
    for j in range(T):
        out_ref[j : j + 1] = f_ref[pl.ds(k * T + j, 1)]
        out_ref[T + j : T + j + 1] = g_ref[pl.ds(k * T + j, 1)]
        out_ref[2 * T + j : 2 * T + j + 1] = d_ref[pl.ds(k * T + j, 1)]
    out_ref[12:13] = a_ref[pl.ds(2 * z + 1, 1)]
    out_ref[13:14] = c_ref[pl.ds(2 * z, 1)]
    out_ref[14:15] = a_ref[pl.ds(2 * z, 1)]
    out_ref[15:16] = c_ref[pl.ds(2 * z + 1, 1)]
    forward, backward = one, one
    earliest, latest = {}, {}
    for d in range(1, chips):
        earliest[d], latest[d] = forward, backward
        before = jnp.maximum(z - d, 0)
        after = jnp.minimum(z + d, chips - 1)
        forward = forward * a_ref[pl.ds(2 * before, 1)] * a_ref[pl.ds(2 * before + 1, 1)]
        backward = backward * c_ref[pl.ds(2 * after, 1)] * c_ref[pl.ds(2 * after + 1, 1)]
    ahead = k % 2 == 0
    for d in range(1, HALF + 1):
        whole = chips - d
        is_forward = jnp.where(jnp.logical_or(ahead, d == HALF), z >= d, z + d >= chips)
        weight = jnp.where(
            jnp.logical_or(ahead, d == HALF),
            jnp.where(is_forward, earliest[d], latest[whole]),
            jnp.where(is_forward, earliest[whole], latest[d]),
        )
        out_ref[15 + d : 16 + d] = jnp.where(is_forward, weight, zero)
        out_ref[19 + d : 20 + d] = jnp.where(is_forward, zero, weight)


def coefficients(gaps):
    years = gaps.shape[0]
    return pl.pallas_call(
        coefficient_kernel,
        in_specs=[pl.BlockSpec(memory_space=pltpu.SMEM)],
        out_specs=vmem(),
        out_shape=sds((24, B), F32),
        scratch_shapes=[pltpu.VMEM((years, B), F32)] * 5 + [pltpu.VMEM((16, B), F32)] * 2,
        compiler_params=PARAMS(),
        cost_estimate=cost(years * B * 200, years * 600),
        name="coefficients",
    )(gaps)


def gradient_kernel(first, *refs):
    n, c, extra = refs[:Q], refs[Q : 2 * Q], refs[2 * Q]
    refs = refs[2 * Q + 1 :]
    if not first:
        w, refs = refs[:Q], refs[Q:]
    gw, gc, coeff_ref = refs[:Q], refs[Q : 2 * Q], refs[2 * Q]
    vocab = Q * Q * B
    for t in range(T):
        panel = jnp.concatenate([r[t] for r in c], 1)
        words = []
        for i in range(Q):
            loaded = word_block(n[i], t).astype(F32)
            block = loaded[:E] if first else w[i][t].astype(F32)
            words.append(block.astype(BF16))
            spare = loaded[E:].T
            negative = (spare[:, 0:1] + spare[:, 1:2]) * (1.0 / vocab)
            scores = jnp.dot(block.T.astype(BF16), panel, preferred_element_type=F32)
            weights = jnp.concatenate([count_block(n[i], t, j) for j in range(Q)], 1).astype(F32)
            half = jnp.tanh(0.5 * scores)
            coeff = 0.5 * ((weights - negative) - (weights + negative) * half)
            coeff_ref[t % 2, i * B : (i + 1) * B, :] = coeff.astype(BF16)
        coeff = coeff_ref[t % 2]
        word_grad = lax.dot_general(
            panel, coeff, (((1,), (1,)), ((), ())), preferred_element_type=F32
        )
        ctx_grad = jnp.dot(jnp.concatenate(words, 1), coeff, preferred_element_type=F32)
        if not first:
            word_grad = jnp.concatenate([word_grad, extra[t]], 0)
            ctx_grad = jnp.concatenate([ctx_grad, jnp.zeros_like(extra[t])], 0)
        word_grad, ctx_grad = word_grad.astype(BF16), ctx_grad.astype(BF16)
        for i in range(Q):
            gw[i][t] = word_grad[:, i * B : (i + 1) * B]
            gc[i][t] = ctx_grad[:, i * B : (i + 1) * B]
    if first:
        for i in range(Q):
            gw[i][T] = extra[0]
            gc[i][T] = extra[1]


def gradients(n, c, extra, w=()):
    first = not w
    return pl.pallas_call(
        functools.partial(gradient_kernel, first),
        in_specs=[vmem()] * (2 * Q + 1 + len(w)),
        out_specs=[vmem()] * (2 * Q),
        out_shape=[sds((T + first, E if first else EP, B), BF16)] * (2 * Q),
        scratch_shapes=[pltpu.VMEM((2, Q * B, Q * B), BF16)],
        compiler_params=PARAMS(),
        cost_estimate=cost(6 * T * 512 * 512 * EP, 6 << 20, 2 * T * 512 * 512),
        name="gradients",
    )(*n, *c, extra, *w)


def entropy(scores):
    size = jnp.abs(scores)
    small = jnp.exp(-size)
    upper = 1.0 / (1.0 + small)
    lower = small * upper
    return jnp.where(scores >= 0, upper, lower), jnp.log(upper) - lower * size


def drift_kernel(*refs):
    n, c, gw, gc = (refs[i * Q : (i + 1) * Q] for i in range(4))
    out_ref, p_ref, h_ref = refs[4 * Q :]
    tiny = jnp.finfo(F32).tiny
    row = lax.broadcasted_iota(jnp.int32, (8, B), 0)
    for i in range(Q):
        for t in range(T + 1):
            if t < T:
                panel = jnp.concatenate([r[t] for r in c], 1)
                block = word_block(n[i], t).astype(F32)[:E]
            else:
                panel = jnp.concatenate([gc[-j % Q][T] for j in range(Q)], 1)
                block = gw[-i % Q][T].astype(F32)
            scores = jnp.dot(block.T.astype(BF16), panel, preferred_element_type=F32)
            p, h = entropy(scores)
            if t > 0:
                m = 0.5 * (p_ref[...] + p)
                rest = 1.0 - m
                mixed = m * jnp.log(jnp.maximum(m, tiny)) + rest * jnp.log(jnp.maximum(rest, tiny))
                js = 0.5 * (h_ref[...] + h) - mixed
                total = js[:, :B] + js[:, B : 2 * B] + js[:, 2 * B : 3 * B] + js[:, 3 * B :]
                total = jnp.sum(total.T, axis=0, keepdims=True)
                high = total.astype(BF16).astype(F32)
                out_ref[t - 1, :, i * B : (i + 1) * B] = jnp.where(
                    row == 0, high, jnp.where(row == 1, total - high, 0.0)
                )
            if t < T:
                p_ref[...] = p
                h_ref[...] = h


def drift_parts(n, c, gw, gc):
    return pl.pallas_call(
        drift_kernel,
        in_specs=[vmem()] * (4 * Q),
        out_specs=vmem(),
        out_shape=sds((T, 8, Q * B), F32),
        scratch_shapes=[pltpu.VMEM((B, Q * B), F32)] * 2,
        compiler_params=PARAMS(),
        cost_estimate=cost(2 * 5 * 512 * 512 * (EP + 30), 4 << 20, 5 * 5 * 512 * 512),
        name="drift",
    )(*n, *c, *gw, *gc)


def summary_kernel(drift, *refs):
    parts = (refs[0:Q], refs[Q : 2 * Q])
    co_ref, b_ref, own_ref = refs[2 * Q : 2 * Q + 3]
    for q in range(2):
        for t in range(T):
            total = parts[q][0][t].astype(F32)
            for r in parts[q][1:]:
                total = total + r[t].astype(F32)
            if drift and q == 0:
                refs[-1][t : t + 1] = total[E : E + 1] + total[E + 1 : E + 2]
            total = total[:E]
            b_ref[q, t] = total
        forward = b_ref[q, 0]
        for t in range(1, T):
            forward = b_ref[q, t] + co_ref[t : t + 1] * forward
        backward = b_ref[q, T - 1]
        for t in reversed(range(T - 1)):
            backward = b_ref[q, t] + co_ref[T + t : T + t + 1] * backward
        own_ref[q] = forward.astype(BF16)
        own_ref[2 + q] = backward.astype(BF16)


def summaries(gw, gc, co, drift):
    return pl.pallas_call(
        functools.partial(summary_kernel, drift),
        in_specs=[vmem()] * (2 * Q + 1),
        out_specs=[vmem()] * (2 + drift),
        out_shape=[sds((2, T, E, B), F32), sds((4, E, B), BF16)] + [sds((T, B), F32)] * drift,
        compiler_params=PARAMS(),
        cost_estimate=cost(2 * T * EP * B * 10, 3 << 20),
        name="summaries",
    )(*gw, *gc, co)


def chip_kernel(own_ref, other_ref, co_ref, *outs):
    k = lax.axis_index("tm")
    even, z = k % 2 == 0, k // 2
    chips = 2 * HALF
    for q in range(2):
        own, other = own_ref[q].astype(F32), other_ref[q].astype(F32)
        forward = jnp.where(even, other, own) + co_ref[12:13] * jnp.where(even, own, other)
        own, other = own_ref[2 + q].astype(F32), other_ref[2 + q].astype(F32)
        backward = jnp.where(even, own, other) + co_ref[13:14] * jnp.where(even, other, own)
        for d in range(1, HALF):
            is_forward = jnp.where(even, z + d < chips, z < d)
            outs[d - 1][q] = jnp.where(is_forward, forward, backward).astype(BF16)

        @pl.when(k % 2 == q)
        def _():
            outs[HALF - 1][...] = jnp.where(z < HALF, forward, backward).astype(BF16)


def chip_summaries(own, other, co):
    return pl.pallas_call(
        chip_kernel,
        in_specs=[vmem()] * 3,
        out_specs=[vmem()] * HALF,
        out_shape=[sds((2, E, B), BF16)] * (HALF - 1) + [sds((E, B), BF16)],
        compiler_params=PARAMS(),
        cost_estimate=cost(EP * B * 16, 1 << 20),
        name="chip_summaries",
    )(own, other, co)


def incoming_kernel(*refs):
    got, co_ref, out_ref = refs[:HALF], refs[HALF], refs[HALF + 1]
    core = lax.axis_index("tm") % 2
    for q in range(2):
        for way in range(2):
            row = 16 + 4 * way
            total = co_ref[row : row + 1] * got[0][q].astype(F32)
            for d in range(2, HALF):
                total = total + co_ref[row + d - 1 : row + d] * got[d - 1][q].astype(F32)
            across = co_ref[row + HALF - 1 : row + HALF] * got[HALF - 1][...].astype(F32)
            total = total + jnp.where(core == q, across, jnp.zeros_like(across))
            out_ref[2 * way + q] = total.astype(BF16)


def incoming(got, co):
    return pl.pallas_call(
        incoming_kernel,
        in_specs=[vmem()] * (HALF + 1),
        out_specs=vmem(),
        out_shape=sds((4, E, B), BF16),
        compiler_params=PARAMS(),
        cost_estimate=cost(4 * EP * B * 8, 1 << 20),
        name="incoming",
    )(*got, co)


def entering(odd, q, near_ref, mine_ref, other_ref, co_ref):
    y = mine_ref[q].astype(F32) + other_ref[q].astype(F32)
    z = mine_ref[2 + q].astype(F32) + other_ref[2 + q].astype(F32)
    y_odd = near_ref[q].astype(F32) + co_ref[14:15] * y
    z_even = near_ref[2 + q].astype(F32) + co_ref[15:16] * z
    return jnp.where(odd, y_odd, y), jnp.where(odd, z, z_even)


def solved_years(b_ref, q, y, z, co_ref):
    ys = []
    for t in range(T):
        y = b_ref[q, t] + co_ref[t : t + 1] * y
        ys.append(y)
    out = [None] * T
    for t in reversed(range(T)):
        carried = co_ref[T + t : T + t + 1] * z
        z = b_ref[q, t] + carried
        out[t] = (ys[t] + carried) * co_ref[2 * T + t : 2 * T + t + 1]
    return out


def update_kernel(scale, b_ref, near_ref, mine_ref, other_ref, co_ref, w_ref, c_ref, *refs):
    odd = lax.axis_index("tm") % 2 == 1
    for q, (old, new) in enumerate(((w_ref, refs[-2]), (c_ref, refs[-1]))):
        y, z = entering(odd, q, near_ref, mine_ref, other_ref, co_ref)
        solved = solved_years(b_ref, q, y, z, co_ref)
        for t in range(T):
            new[t] = (old[t].astype(F32) + scale * solved[t]).astype(BF16)


def finish_kernel(scale, vocab, *refs):
    *ins, raw_ref, nw_ref, nc_ref, drift_ref = refs
    update_kernel(scale, *ins, nw_ref, nc_ref)
    last = lax.axis_index("tm") == lax.axis_size("tm") - 1
    drift = raw_ref[...] * (float(vocab) ** -0.5)
    at = lax.broadcasted_iota(jnp.int32, (T, B), 0)
    drift_ref[...] = jnp.where(jnp.logical_and(last, at == T - 1), 0.0, drift)


def update(scale, *arrays):
    return pl.pallas_call(
        functools.partial(update_kernel, scale),
        in_specs=[vmem()] * 7,
        out_specs=[vmem()] * 2,
        out_shape=[sds((T, E, B), BF16)] * 2,
        compiler_params=PARAMS(),
        cost_estimate=cost(2 * T * EP * B * 10, 3 << 20),
        name="update",
    )(*arrays)


def finish(scale, vocab, *arrays):
    return pl.pallas_call(
        functools.partial(finish_kernel, scale, vocab),
        in_specs=[vmem()] * 8,
        out_specs=[vmem()] * 3,
        out_shape=[sds((T, E, B), BF16)] * 2 + [sds((T, B), F32)],
        compiler_params=PARAMS(),
        cost_estimate=cost(2 * T * EP * B * 10, 3 << 20),
        name="finish",
    )(*arrays)


def step(v, s, rows):
    y, x = v // Q, v % Q
    return y * Q + (x + s) % Q if rows else ((y + s) % Q) * Q + x


def in_grid(a, s, of_words):
    years, places = lax.axis_size("tm"), Q * Q
    pairs = [
        (k * places + v, k * places + step(v, s, (k % 2 == 0) == of_words))
        for k in range(years)
        for v in range(places)
    ]
    return lax.ppermute(a, ("tm", "vocab"), pairs)


def other_core(a):
    return lax.ppermute(a, "tm", [(k, k ^ 1) for k in range(lax.axis_size("tm"))])


def along_z(a, d):
    chips = lax.axis_size("tm") // 2
    ahead = [(2 * z, 2 * ((z + d) % chips)) for z in range(chips)]
    back = [(2 * z + 1, 2 * ((z - d) % chips) + 1) for z in range(chips)]
    return lax.ppermute(a, "tm", ahead + back)


def from_next(a):
    return lax.ppermute(a, "tm", [(k, k - 1) for k in range(1, lax.axis_size("tm"))])


ORDER = (1, 2, 3)


def spread(words, contexts):
    w, c = {0: words[0]}, {0: contexts[0]}
    for s in ORDER:
        w[s] = in_grid(words[s], s, True)
        c[s] = in_grid(contexts[s], s, False)
    return [w[s] for s in range(Q)], [c[s] for s in range(Q)]


def collected(words, contexts):
    w, c = {0: words[0]}, {0: contexts[0]}
    for s in ORDER:
        w[s] = in_grid(words[s], -s, True)
        c[s] = in_grid(contexts[s], -s, False)
    return [w[s] for s in range(Q)], [c[s] for s in range(Q)]


def on_device(counts, word_vecs, ctx_vecs, gaps):
    vocab = counts.shape[2]
    scale = RATE / float(vocab) ** 0.5
    words, contexts = word_vecs.transpose(0, 2, 1), ctx_vecs.transpose(0, 2, 1)
    loads = stage(counts, words)
    n, c = spread(loads, [contexts] * Q)
    following = from_next(jnp.stack([words[0], contexts[0]], 0))
    co = coefficients(gaps)
    w, extra = (), following
    for sweep in range(SWEEPS):
        last = sweep == SWEEPS - 1
        if sweep:
            w, c = spread([words] * Q, [contexts] * Q)
        grads = gradients(n, c, extra, w)
        gw, gc = collected(grads[:Q], grads[Q:])
        b, own, *raw = summaries(gw, gc, co, last)
        near = other_core(own)
        outs = chip_summaries(own, near, co)
        if sweep == 0:
            outs, held = lax.optimization_barrier((outs, c))
            extra = drift_parts(n, held, gw, gc)
        got = {d: along_z(outs[d - 1], d) for d in (4, 3, 2, 1)}
        got = [got[d] for d in range(1, HALF + 1)]
        if sweep == 0:
            got, extra = lax.optimization_barrier((got, extra))
        mine = incoming(got, co)
        other = other_core(mine)
        if last:
            words, contexts, drift = finish(
                scale, vocab, b, near, mine, other, co, words, contexts, *raw
            )
            return (words.transpose(0, 2, 1), contexts.transpose(0, 2, 1), drift)
        words, contexts = update(scale, b, near, mine, other, co, words, contexts)


def solution(mesh):
    return jax.shard_map(
        on_device,
        mesh=mesh,
        in_specs=(P("tm", "vocab", None), P("tm", "vocab", None), P("tm", "vocab", None), P()),
        out_specs=(P("tm", "vocab", None), P("tm", "vocab", None), P("tm", "vocab")),
        check_vma=False,
    )
```

```python
import functools

import jax
import jax.numpy as jnp
from jax import lax
from jax.experimental import pallas as pl
from jax.experimental.pallas import tpu as pltpu
from jax.sharding import PartitionSpec as P

PRIOR = 0.05
DIFF = 0.5
RATE = 0.2
SWEEPS = 2


E = 200
EP = 208
B = 128
T = 4
Q = 4
HALF = 4
F32 = jnp.float32
BF16 = jnp.bfloat16

PARAMS = functools.partial(pltpu.CompilerParams, vmem_limit_bytes=24 * 1024 * 1024)


def sds(shape, dtype):
    return jax.ShapeDtypeStruct(shape, dtype)


def vmem():
    return pl.BlockSpec(memory_space=pltpu.VMEM)


def cost(flops, moved, special=0):
    return pl.CostEstimate(flops=int(flops), bytes_accessed=int(moved), transcendentals=int(special))


COUNT_ROWS = T * Q * B
ROWS = COUNT_ROWS + T * EP


def count_block(ref, t, j):
    at = (t * Q + j) * B
    return ref[at : at + B]


def word_block(ref, t):
    at = COUNT_ROWS + t * EP
    return ref[at : at + EP]


def stage_kernel(counts_ref, w_ref, *loads):
    along_rows = lax.axis_index("tm") % 2 == 0
    place = lax.axis_index("vocab")
    y, x = place // Q, place % Q
    row = lax.broadcasted_iota(jnp.int32, (8, B), 0)
    ones = jnp.ones((8, B), BF16)
    for t in range(T):
        total = jnp.zeros((8, B), F32)
        for s in range(Q):
            for j in range(Q):
                block = jnp.where(
                    along_rows,
                    ((y + Q - j) % Q) * Q + (x + s) % Q,
                    ((y + s) % Q) * Q + (x + Q - j) % Q,
                )
                at = pl.multiple_of(block * B, B)
                to = (t * Q + j) * B
                part = counts_ref[t, :, pl.ds(at, B)].astype(F32).astype(BF16)
                loads[s][to : to + B] = part
                total = total + lax.dot_general(
                    ones, part, (((1,), (1,)), ((), ())), preferred_element_type=F32
                )
        high = total.astype(BF16).astype(F32)
        spare = jnp.where(row == 0, high, jnp.where(row == 1, total - high, 0.0))
        word = jnp.concatenate([w_ref[t].astype(F32), spare], 0).astype(BF16)
        for s in range(Q):
            loads[s][COUNT_ROWS + t * EP : COUNT_ROWS + (t + 1) * EP] = word


def stage(counts, words):
    vocab = counts.shape[2]
    return pl.pallas_call(
        stage_kernel,
        in_specs=[vmem()] * 2,
        out_specs=[vmem()] * Q,
        out_shape=[sds((ROWS, B), BF16)] * Q,
        compiler_params=PARAMS(),
        cost_estimate=cost(T * B * vocab * 16, T * B * vocab * 6),
        name="stage",
    )(counts, words)


def coefficient_kernel(gaps_ref, out_ref, link_ref, f_ref, g_ref, d_ref, e_ref, a_ref, c_ref):
    years = gaps_ref.shape[0]
    chips = years // (2 * T)
    one = jnp.ones((1, B), F32)
    zero = jnp.zeros((1, B), F32)
    for t in range(years - 1):
        link_ref[t : t + 1] = one / (DIFF * (one * gaps_ref[t].astype(F32)))

    def link(t):
        return link_ref[t : t + 1] if 0 <= t < years - 1 else zero

    def diagonal(t):
        return PRIOR + link(t - 1) + link(t)

    delta, eps = diagonal(0), diagonal(years - 1)
    f_ref[0:1] = zero
    g_ref[years - 1 : years] = zero
    d_ref[0:1] = delta
    e_ref[years - 1 : years] = eps
    for t in range(1, years):
        f = link(t - 1) / delta
        delta = diagonal(t) - link(t - 1) * f
        f_ref[t : t + 1] = f
        d_ref[t : t + 1] = delta
        u = years - 1 - t
        g = link(u) / eps
        eps = diagonal(u) - link(u) * g
        g_ref[u : u + 1] = g
        e_ref[u : u + 1] = eps
    for t in range(years):
        d_ref[t : t + 1] = one / (d_ref[t : t + 1] + e_ref[t : t + 1] - diagonal(t))
    for k in range(2 * chips):
        fs, gs = f_ref[k * T : k * T + 1], g_ref[k * T : k * T + 1]
        for j in range(1, T):
            fs = fs * f_ref[k * T + j : k * T + j + 1]
            gs = gs * g_ref[k * T + j : k * T + j + 1]
        a_ref[k : k + 1] = fs
        c_ref[k : k + 1] = gs
    k = lax.axis_index("tm")
    z = k // 2
    for j in range(T):
        out_ref[j : j + 1] = f_ref[pl.ds(k * T + j, 1)]
        out_ref[T + j : T + j + 1] = g_ref[pl.ds(k * T + j, 1)]
        out_ref[2 * T + j : 2 * T + j + 1] = d_ref[pl.ds(k * T + j, 1)]
    out_ref[12:13] = a_ref[pl.ds(2 * z + 1, 1)]
    out_ref[13:14] = c_ref[pl.ds(2 * z, 1)]
    out_ref[14:15] = a_ref[pl.ds(2 * z, 1)]
    out_ref[15:16] = c_ref[pl.ds(2 * z + 1, 1)]
    forward, backward = one, one
    earliest, latest = {}, {}
    for d in range(1, chips):
        earliest[d], latest[d] = forward, backward
        before = jnp.maximum(z - d, 0)
        after = jnp.minimum(z + d, chips - 1)
        forward = forward * a_ref[pl.ds(2 * before, 1)] * a_ref[pl.ds(2 * before + 1, 1)]
        backward = backward * c_ref[pl.ds(2 * after, 1)] * c_ref[pl.ds(2 * after + 1, 1)]
    ahead = k % 2 == 0
    for d in range(1, HALF + 1):
        whole = chips - d
        is_forward = jnp.where(jnp.logical_or(ahead, d == HALF), z >= d, z + d >= chips)
        weight = jnp.where(
            jnp.logical_or(ahead, d == HALF),
            jnp.where(is_forward, earliest[d], latest[whole]),
            jnp.where(is_forward, earliest[whole], latest[d]),
        )
        out_ref[15 + d : 16 + d] = jnp.where(is_forward, weight, zero)
        out_ref[19 + d : 20 + d] = jnp.where(is_forward, zero, weight)


def coefficients(gaps):
    years = gaps.shape[0]
    return pl.pallas_call(
        coefficient_kernel,
        in_specs=[pl.BlockSpec(memory_space=pltpu.SMEM)],
        out_specs=vmem(),
        out_shape=sds((24, B), F32),
        scratch_shapes=[pltpu.VMEM((years, B), F32)] * 5 + [pltpu.VMEM((16, B), F32)] * 2,
        compiler_params=PARAMS(),
        cost_estimate=cost(years * B * 200, years * 600),
        name="coefficients",
    )(gaps)


def gradient_kernel(first, *refs):
    n, c, extra = refs[:Q], refs[Q : 2 * Q], refs[2 * Q]
    refs = refs[2 * Q + 1 :]
    if not first:
        w, refs = refs[:Q], refs[Q:]
    gw, gc, coeff_ref = refs[:Q], refs[Q : 2 * Q], refs[2 * Q]
    vocab = Q * Q * B
    for t in range(T):
        panel = jnp.concatenate([r[t] for r in c], 1)
        words = []
        for i in range(Q):
            loaded = word_block(n[i], t).astype(F32)
            block = loaded[:E] if first else w[i][t].astype(F32)
            words.append(block.astype(BF16))
            spare = loaded[E:].T
            negative = (spare[:, 0:1] + spare[:, 1:2]) * (1.0 / vocab)
            scores = jnp.dot(block.T.astype(BF16), panel, preferred_element_type=F32)
            weights = jnp.concatenate([count_block(n[i], t, j) for j in range(Q)], 1).astype(F32)
            half = jnp.tanh(0.5 * scores)
            coeff = 0.5 * ((weights - negative) - (weights + negative) * half)
            coeff_ref[t % 2, i * B : (i + 1) * B, :] = coeff.astype(BF16)
        coeff = coeff_ref[t % 2]
        word_grad = lax.dot_general(
            panel, coeff, (((1,), (1,)), ((), ())), preferred_element_type=F32
        )
        ctx_grad = jnp.dot(jnp.concatenate(words, 1), coeff, preferred_element_type=F32)
        if not first:
            word_grad = jnp.concatenate([word_grad, extra[t]], 0)
            ctx_grad = jnp.concatenate([ctx_grad, jnp.zeros_like(extra[t])], 0)
        word_grad, ctx_grad = word_grad.astype(BF16), ctx_grad.astype(BF16)
        for i in range(Q):
            gw[i][t] = word_grad[:, i * B : (i + 1) * B]
            gc[i][t] = ctx_grad[:, i * B : (i + 1) * B]
    if first:
        for i in range(Q):
            gw[i][T] = extra[0]
            gc[i][T] = extra[1]


def gradients(n, c, extra, w=()):
    first = not w
    return pl.pallas_call(
        functools.partial(gradient_kernel, first),
        in_specs=[vmem()] * (2 * Q + 1 + len(w)),
        out_specs=[vmem()] * (2 * Q),
        out_shape=[sds((T + first, E if first else EP, B), BF16)] * (2 * Q),
        scratch_shapes=[pltpu.VMEM((2, Q * B, Q * B), BF16)],
        compiler_params=PARAMS(),
        cost_estimate=cost(6 * T * 512 * 512 * EP, 6 << 20, 2 * T * 512 * 512),
        name="gradients",
    )(*n, *c, extra, *w)


def entropy(scores):
    size = jnp.abs(scores)
    small = jnp.exp(-size)
    upper = 1.0 / (1.0 + small)
    lower = small * upper
    return jnp.where(scores >= 0, upper, lower), jnp.log(upper) - lower * size


def drift_kernel(*refs):
    n, c, gw, gc = (refs[i * Q : (i + 1) * Q] for i in range(4))
    out_ref, p_ref, h_ref = refs[4 * Q :]
    tiny = jnp.finfo(F32).tiny
    row = lax.broadcasted_iota(jnp.int32, (8, B), 0)
    for i in range(Q):
        for t in range(T + 1):
            if t < T:
                panel = jnp.concatenate([r[t] for r in c], 1)
                block = word_block(n[i], t).astype(F32)[:E]
            else:
                panel = jnp.concatenate([gc[-j % Q][T] for j in range(Q)], 1)
                block = gw[-i % Q][T].astype(F32)
            scores = jnp.dot(block.T.astype(BF16), panel, preferred_element_type=F32)
            p, h = entropy(scores)
            if t > 0:
                m = 0.5 * (p_ref[...] + p)
                rest = 1.0 - m
                mixed = m * jnp.log(jnp.maximum(m, tiny)) + rest * jnp.log(jnp.maximum(rest, tiny))
                js = 0.5 * (h_ref[...] + h) - mixed
                total = js[:, :B] + js[:, B : 2 * B] + js[:, 2 * B : 3 * B] + js[:, 3 * B :]
                total = jnp.sum(total.T, axis=0, keepdims=True)
                high = total.astype(BF16).astype(F32)
                out_ref[t - 1, :, i * B : (i + 1) * B] = jnp.where(
                    row == 0, high, jnp.where(row == 1, total - high, 0.0)
                )
            if t < T:
                p_ref[...] = p
                h_ref[...] = h


def drift_parts(n, c, gw, gc):
    return pl.pallas_call(
        drift_kernel,
        in_specs=[vmem()] * (4 * Q),
        out_specs=vmem(),
        out_shape=sds((T, 8, Q * B), F32),
        scratch_shapes=[pltpu.VMEM((B, Q * B), F32)] * 2,
        compiler_params=PARAMS(),
        cost_estimate=cost(2 * 5 * 512 * 512 * (EP + 30), 4 << 20, 5 * 5 * 512 * 512),
        name="drift",
    )(*n, *c, *gw, *gc)


def summary_kernel(drift, *refs):
    parts = (refs[0:Q], refs[Q : 2 * Q])
    co_ref, b_ref, own_ref = refs[2 * Q : 2 * Q + 3]
    for q in range(2):
        for t in range(T):
            total = parts[q][0][t].astype(F32)
            for r in parts[q][1:]:
                total = total + r[t].astype(F32)
            if drift and q == 0:
                refs[-1][t : t + 1] = total[E : E + 1] + total[E + 1 : E + 2]
            total = total[:E]
            b_ref[q, t] = total
        forward = b_ref[q, 0]
        for t in range(1, T):
            forward = b_ref[q, t] + co_ref[t : t + 1] * forward
        backward = b_ref[q, T - 1]
        for t in reversed(range(T - 1)):
            backward = b_ref[q, t] + co_ref[T + t : T + t + 1] * backward
        own_ref[q] = forward.astype(BF16)
        own_ref[2 + q] = backward.astype(BF16)


def summaries(gw, gc, co, drift):
    return pl.pallas_call(
        functools.partial(summary_kernel, drift),
        in_specs=[vmem()] * (2 * Q + 1),
        out_specs=[vmem()] * (2 + drift),
        out_shape=[sds((2, T, E, B), F32), sds((4, E, B), BF16)] + [sds((T, B), F32)] * drift,
        compiler_params=PARAMS(),
        cost_estimate=cost(2 * T * EP * B * 10, 3 << 20),
        name="summaries",
    )(*gw, *gc, co)


def chip_kernel(own_ref, other_ref, co_ref, *outs):
    k = lax.axis_index("tm")
    even, z = k % 2 == 0, k // 2
    chips = 2 * HALF
    for q in range(2):
        own, other = own_ref[q].astype(F32), other_ref[q].astype(F32)
        forward = jnp.where(even, other, own) + co_ref[12:13] * jnp.where(even, own, other)
        own, other = own_ref[2 + q].astype(F32), other_ref[2 + q].astype(F32)
        backward = jnp.where(even, own, other) + co_ref[13:14] * jnp.where(even, other, own)
        for d in range(1, HALF):
            is_forward = jnp.where(even, z + d < chips, z < d)
            outs[d - 1][q] = jnp.where(is_forward, forward, backward).astype(BF16)

        @pl.when(k % 2 == q)
        def _():
            outs[HALF - 1][...] = jnp.where(z < HALF, forward, backward).astype(BF16)


def chip_summaries(own, other, co):
    return pl.pallas_call(
        chip_kernel,
        in_specs=[vmem()] * 3,
        out_specs=[vmem()] * HALF,
        out_shape=[sds((2, E, B), BF16)] * (HALF - 1) + [sds((E, B), BF16)],
        compiler_params=PARAMS(),
        cost_estimate=cost(EP * B * 16, 1 << 20),
        name="chip_summaries",
    )(own, other, co)


def incoming_kernel(*refs):
    got, co_ref, out_ref = refs[:HALF], refs[HALF], refs[HALF + 1]
    core = lax.axis_index("tm") % 2
    for q in range(2):
        for way in range(2):
            row = 16 + 4 * way
            total = co_ref[row : row + 1] * got[0][q].astype(F32)
            for d in range(2, HALF):
                total = total + co_ref[row + d - 1 : row + d] * got[d - 1][q].astype(F32)
            across = co_ref[row + HALF - 1 : row + HALF] * got[HALF - 1][...].astype(F32)
            total = total + jnp.where(core == q, across, jnp.zeros_like(across))
            out_ref[2 * way + q] = total.astype(BF16)


def incoming(got, co):
    return pl.pallas_call(
        incoming_kernel,
        in_specs=[vmem()] * (HALF + 1),
        out_specs=vmem(),
        out_shape=sds((4, E, B), BF16),
        compiler_params=PARAMS(),
        cost_estimate=cost(4 * EP * B * 8, 1 << 20),
        name="incoming",
    )(*got, co)


def entering(odd, q, near_ref, mine_ref, other_ref, co_ref):
    y = mine_ref[q].astype(F32) + other_ref[q].astype(F32)
    z = mine_ref[2 + q].astype(F32) + other_ref[2 + q].astype(F32)
    y_odd = near_ref[q].astype(F32) + co_ref[14:15] * y
    z_even = near_ref[2 + q].astype(F32) + co_ref[15:16] * z
    return jnp.where(odd, y_odd, y), jnp.where(odd, z, z_even)


def solved_years(b_ref, q, y, z, co_ref):
    ys = []
    for t in range(T):
        y = b_ref[q, t] + co_ref[t : t + 1] * y
        ys.append(y)
    out = [None] * T
    for t in reversed(range(T)):
        carried = co_ref[T + t : T + t + 1] * z
        z = b_ref[q, t] + carried
        out[t] = (ys[t] + carried) * co_ref[2 * T + t : 2 * T + t + 1]
    return out


def update_kernel(scale, b_ref, near_ref, mine_ref, other_ref, co_ref, w_ref, c_ref, *refs):
    odd = lax.axis_index("tm") % 2 == 1
    for q, (old, new) in enumerate(((w_ref, refs[-2]), (c_ref, refs[-1]))):
        y, z = entering(odd, q, near_ref, mine_ref, other_ref, co_ref)
        solved = solved_years(b_ref, q, y, z, co_ref)
        for t in range(T):
            new[t] = (old[t].astype(F32) + scale * solved[t]).astype(BF16)


def finish_kernel(scale, vocab, *refs):
    *ins, raw_ref, nw_ref, nc_ref, drift_ref = refs
    update_kernel(scale, *ins, nw_ref, nc_ref)
    last = lax.axis_index("tm") == lax.axis_size("tm") - 1
    drift = raw_ref[...] * (float(vocab) ** -0.5)
    at = lax.broadcasted_iota(jnp.int32, (T, B), 0)
    drift_ref[...] = jnp.where(jnp.logical_and(last, at == T - 1), 0.0, drift)


def update(scale, *arrays):
    return pl.pallas_call(
        functools.partial(update_kernel, scale),
        in_specs=[vmem()] * 7,
        out_specs=[vmem()] * 2,
        out_shape=[sds((T, E, B), BF16)] * 2,
        compiler_params=PARAMS(),
        cost_estimate=cost(2 * T * EP * B * 10, 3 << 20),
        name="update",
    )(*arrays)


def finish(scale, vocab, *arrays):
    return pl.pallas_call(
        functools.partial(finish_kernel, scale, vocab),
        in_specs=[vmem()] * 8,
        out_specs=[vmem()] * 3,
        out_shape=[sds((T, E, B), BF16)] * 2 + [sds((T, B), F32)],
        compiler_params=PARAMS(),
        cost_estimate=cost(2 * T * EP * B * 10, 3 << 20),
        name="finish",
    )(*arrays)


def step(v, s, rows):
    y, x = v // Q, v % Q
    return y * Q + (x + s) % Q if rows else ((y + s) % Q) * Q + x


def in_grid(a, s, of_words):
    years, places = lax.axis_size("tm"), Q * Q
    pairs = [
        (k * places + v, k * places + step(v, s, (k % 2 == 0) == of_words))
        for k in range(years)
        for v in range(places)
    ]
    return lax.ppermute(a, ("tm", "vocab"), pairs)


def other_core(a):
    return lax.ppermute(a, "tm", [(k, k ^ 1) for k in range(lax.axis_size("tm"))])


def along_z(a, d):
    chips = lax.axis_size("tm") // 2
    ahead = [(2 * z, 2 * ((z + d) % chips)) for z in range(chips)]
    back = [(2 * z + 1, 2 * ((z - d) % chips) + 1) for z in range(chips)]
    return lax.ppermute(a, "tm", ahead + back)


def from_next(a):
    return lax.ppermute(a, "tm", [(k, k - 1) for k in range(1, lax.axis_size("tm"))])


ORDER = (1, 2, 3)


def spread(words, contexts):
    w, c = {0: words[0]}, {0: contexts[0]}
    for s in ORDER:
        w[s] = in_grid(words[s], s, True)
        c[s] = in_grid(contexts[s], s, False)
    return [w[s] for s in range(Q)], [c[s] for s in range(Q)]


def collected(words, contexts):
    w, c = {0: words[0]}, {0: contexts[0]}
    for s in ORDER:
        w[s] = in_grid(words[s], -s, True)
        c[s] = in_grid(contexts[s], -s, False)
    return [w[s] for s in range(Q)], [c[s] for s in range(Q)]


def on_device(counts, word_vecs, ctx_vecs, gaps):
    vocab = counts.shape[2]
    scale = RATE / float(vocab) ** 0.5
    words, contexts = word_vecs.transpose(0, 2, 1), ctx_vecs.transpose(0, 2, 1)
    loads = stage(counts, words)
    n, c = spread(loads, [contexts] * Q)
    held, c[1] = lax.optimization_barrier((jnp.stack([words[0], contexts[0]], 0), c[1]))
    following = from_next(held)
    co = coefficients(gaps)
    w, extra = (), following
    for sweep in range(SWEEPS):
        last = sweep == SWEEPS - 1
        if sweep:
            w, c = spread([words] * Q, [contexts] * Q)
        grads = gradients(n, c, extra, w)
        gw, gc = collected(grads[:Q], grads[Q:])
        b, own, *raw = summaries(gw, gc, co, last)
        near = other_core(own)
        outs = chip_summaries(own, near, co)
        if sweep == 0:
            outs, held = lax.optimization_barrier((outs, c))
            extra = drift_parts(n, held, gw, gc)
        got = {d: along_z(outs[d - 1], d) for d in (4, 3, 2, 1)}
        got = [got[d] for d in range(1, HALF + 1)]
        if sweep == 0:
            got, extra = lax.optimization_barrier((got, extra))
        mine = incoming(got, co)
        other = other_core(mine)
        if last:
            words, contexts, drift = finish(
                scale, vocab, b, near, mine, other, co, words, contexts, *raw
            )
            return (words.transpose(0, 2, 1), contexts.transpose(0, 2, 1), drift)
        words, contexts = update(scale, b, near, mine, other, co, words, contexts)


def solution(mesh):
    return jax.shard_map(
        on_device,
        mesh=mesh,
        in_specs=(P("tm", "vocab", None), P("tm", "vocab", None), P("tm", "vocab", None), P()),
        out_specs=(P("tm", "vocab", None), P("tm", "vocab", None), P("tm", "vocab")),
        check_vma=False,
    )
```

```python
import functools

import jax
import jax.numpy as jnp
from jax import lax
from jax.experimental import pallas as pl
from jax.experimental.pallas import tpu as pltpu
from jax.sharding import PartitionSpec as P

PRIOR = 0.05
DIFF = 0.5
RATE = 0.2
SWEEPS = 2


E = 200
EP = 208
B = 128
T = 4
Q = 4
HALF = 4
F32 = jnp.float32
BF16 = jnp.bfloat16

PARAMS = functools.partial(pltpu.CompilerParams, vmem_limit_bytes=24 * 1024 * 1024)


def sds(shape, dtype):
    return jax.ShapeDtypeStruct(shape, dtype)


def vmem():
    return pl.BlockSpec(memory_space=pltpu.VMEM)


def cost(flops, moved, special=0):
    return pl.CostEstimate(flops=int(flops), bytes_accessed=int(moved), transcendentals=int(special))


COUNT_ROWS = T * Q * B
ROWS = COUNT_ROWS + T * EP


def count_block(ref, t, j):
    at = (t * Q + j) * B
    return ref[at : at + B]


def word_block(ref, t):
    at = COUNT_ROWS + t * EP
    return ref[at : at + EP]


def stage_kernel(counts_ref, w_ref, *loads):
    along_rows = lax.axis_index("tm") % 2 == 0
    place = lax.axis_index("vocab")
    y, x = place // Q, place % Q
    row = lax.broadcasted_iota(jnp.int32, (8, B), 0)
    ones = jnp.ones((8, B), BF16)
    for t in range(T):
        total = jnp.zeros((8, B), F32)
        for s in range(Q):
            for j in range(Q):
                block = jnp.where(
                    along_rows,
                    ((y + Q - j) % Q) * Q + (x + s) % Q,
                    ((y + s) % Q) * Q + (x + Q - j) % Q,
                )
                at = pl.multiple_of(block * B, B)
                to = (t * Q + j) * B
                part = counts_ref[t, :, pl.ds(at, B)].astype(F32).astype(BF16)
                loads[s][to : to + B] = part
                total = total + lax.dot_general(
                    ones, part, (((1,), (1,)), ((), ())), preferred_element_type=F32
                )
        high = total.astype(BF16).astype(F32)
        spare = jnp.where(row == 0, high, jnp.where(row == 1, total - high, 0.0))
        word = jnp.concatenate([w_ref[t].astype(F32), spare], 0).astype(BF16)
        for s in range(Q):
            loads[s][COUNT_ROWS + t * EP : COUNT_ROWS + (t + 1) * EP] = word


def stage(counts, words):
    vocab = counts.shape[2]
    return pl.pallas_call(
        stage_kernel,
        in_specs=[vmem()] * 2,
        out_specs=[vmem()] * Q,
        out_shape=[sds((ROWS, B), BF16)] * Q,
        compiler_params=PARAMS(),
        cost_estimate=cost(T * B * vocab * 16, T * B * vocab * 6),
        name="stage",
    )(counts, words)


def coefficient_kernel(gaps_ref, out_ref, link_ref, f_ref, g_ref, d_ref, e_ref, a_ref, c_ref):
    years = gaps_ref.shape[0]
    chips = years // (2 * T)
    one = jnp.ones((1, B), F32)
    zero = jnp.zeros((1, B), F32)
    for t in range(years - 1):
        link_ref[t : t + 1] = one / (DIFF * (one * gaps_ref[t].astype(F32)))

    def link(t):
        return link_ref[t : t + 1] if 0 <= t < years - 1 else zero

    def diagonal(t):
        return PRIOR + link(t - 1) + link(t)

    delta, eps = diagonal(0), diagonal(years - 1)
    f_ref[0:1] = zero
    g_ref[years - 1 : years] = zero
    d_ref[0:1] = delta
    e_ref[years - 1 : years] = eps
    for t in range(1, years):
        f = link(t - 1) / delta
        delta = diagonal(t) - link(t - 1) * f
        f_ref[t : t + 1] = f
        d_ref[t : t + 1] = delta
        u = years - 1 - t
        g = link(u) / eps
        eps = diagonal(u) - link(u) * g
        g_ref[u : u + 1] = g
        e_ref[u : u + 1] = eps
    for t in range(years):
        d_ref[t : t + 1] = one / (d_ref[t : t + 1] + e_ref[t : t + 1] - diagonal(t))
    for k in range(2 * chips):
        fs, gs = f_ref[k * T : k * T + 1], g_ref[k * T : k * T + 1]
        for j in range(1, T):
            fs = fs * f_ref[k * T + j : k * T + j + 1]
            gs = gs * g_ref[k * T + j : k * T + j + 1]
        a_ref[k : k + 1] = fs
        c_ref[k : k + 1] = gs
    k = lax.axis_index("tm")
    z = k // 2
    for j in range(T):
        out_ref[j : j + 1] = f_ref[pl.ds(k * T + j, 1)]
        out_ref[T + j : T + j + 1] = g_ref[pl.ds(k * T + j, 1)]
        out_ref[2 * T + j : 2 * T + j + 1] = d_ref[pl.ds(k * T + j, 1)]
    out_ref[12:13] = a_ref[pl.ds(2 * z + 1, 1)]
    out_ref[13:14] = c_ref[pl.ds(2 * z, 1)]
    out_ref[14:15] = a_ref[pl.ds(2 * z, 1)]
    out_ref[15:16] = c_ref[pl.ds(2 * z + 1, 1)]
    forward, backward = one, one
    earliest, latest = {}, {}
    for d in range(1, chips):
        earliest[d], latest[d] = forward, backward
        before = jnp.maximum(z - d, 0)
        after = jnp.minimum(z + d, chips - 1)
        forward = forward * a_ref[pl.ds(2 * before, 1)] * a_ref[pl.ds(2 * before + 1, 1)]
        backward = backward * c_ref[pl.ds(2 * after, 1)] * c_ref[pl.ds(2 * after + 1, 1)]
    ahead = k % 2 == 0
    for d in range(1, HALF + 1):
        whole = chips - d
        is_forward = jnp.where(jnp.logical_or(ahead, d == HALF), z >= d, z + d >= chips)
        weight = jnp.where(
            jnp.logical_or(ahead, d == HALF),
            jnp.where(is_forward, earliest[d], latest[whole]),
            jnp.where(is_forward, earliest[whole], latest[d]),
        )
        out_ref[15 + d : 16 + d] = jnp.where(is_forward, weight, zero)
        out_ref[19 + d : 20 + d] = jnp.where(is_forward, zero, weight)


def coefficients(gaps):
    years = gaps.shape[0]
    return pl.pallas_call(
        coefficient_kernel,
        in_specs=[pl.BlockSpec(memory_space=pltpu.SMEM)],
        out_specs=vmem(),
        out_shape=sds((24, B), F32),
        scratch_shapes=[pltpu.VMEM((years, B), F32)] * 5 + [pltpu.VMEM((16, B), F32)] * 2,
        compiler_params=PARAMS(),
        cost_estimate=cost(years * B * 200, years * 600),
        name="coefficients",
    )(gaps)


def gradient_kernel(first, *refs):
    n, c, extra = refs[:Q], refs[Q : 2 * Q], refs[2 * Q]
    refs = refs[2 * Q + 1 :]
    if not first:
        w, refs = refs[:Q], refs[Q:]
    gw, gc, coeff_ref = refs[:Q], refs[Q : 2 * Q], refs[2 * Q]
    vocab = Q * Q * B
    for t in range(T):
        panel = jnp.concatenate([r[t] for r in c], 1)
        words = []
        for i in range(Q):
            loaded = word_block(n[i], t).astype(F32)
            block = loaded[:E] if first else w[i][t].astype(F32)
            words.append(block.astype(BF16))
            spare = loaded[E:].T
            negative = (spare[:, 0:1] + spare[:, 1:2]) * (1.0 / vocab)
            scores = jnp.dot(block.T.astype(BF16), panel, preferred_element_type=F32)
            weights = jnp.concatenate([count_block(n[i], t, j) for j in range(Q)], 1).astype(F32)
            half = jnp.tanh(0.5 * scores)
            coeff = 0.5 * ((weights - negative) - (weights + negative) * half)
            coeff_ref[t % 2, i * B : (i + 1) * B, :] = coeff.astype(BF16)
        coeff = coeff_ref[t % 2]
        word_grad = lax.dot_general(
            panel, coeff, (((1,), (1,)), ((), ())), preferred_element_type=F32
        )
        ctx_grad = jnp.dot(jnp.concatenate(words, 1), coeff, preferred_element_type=F32)
        if not first:
            word_grad = jnp.concatenate([word_grad, extra[t]], 0)
            ctx_grad = jnp.concatenate([ctx_grad, jnp.zeros_like(extra[t])], 0)
        word_grad, ctx_grad = word_grad.astype(BF16), ctx_grad.astype(BF16)
        for i in range(Q):
            gw[i][t] = word_grad[:, i * B : (i + 1) * B]
            gc[i][t] = ctx_grad[:, i * B : (i + 1) * B]
    if first:
        for i in range(Q):
            gw[i][T] = extra[0]
            gc[i][T] = extra[1]


def gradients(n, c, extra, w=()):
    first = not w
    return pl.pallas_call(
        functools.partial(gradient_kernel, first),
        in_specs=[vmem()] * (2 * Q + 1 + len(w)),
        out_specs=[vmem()] * (2 * Q),
        out_shape=[sds((T + first, E if first else EP, B), BF16)] * (2 * Q),
        scratch_shapes=[pltpu.VMEM((2, Q * B, Q * B), BF16)],
        compiler_params=PARAMS(),
        cost_estimate=cost(6 * T * 512 * 512 * EP, 6 << 20, 2 * T * 512 * 512),
        name="gradients",
    )(*n, *c, extra, *w)


def entropy(scores):
    size = jnp.abs(scores)
    small = jnp.exp(-size)
    upper = 1.0 / (1.0 + small)
    lower = small * upper
    return jnp.where(scores >= 0, upper, lower), jnp.log(upper) - lower * size


def drift_kernel(*refs):
    n, c, gw, gc = (refs[i * Q : (i + 1) * Q] for i in range(4))
    out_ref, p_ref, h_ref = refs[4 * Q :]
    tiny = jnp.finfo(F32).tiny
    row = lax.broadcasted_iota(jnp.int32, (8, B), 0)
    for i in range(Q):
        for t in range(T + 1):
            if t < T:
                panel = jnp.concatenate([r[t] for r in c], 1)
                block = word_block(n[i], t).astype(F32)[:E]
            else:
                panel = jnp.concatenate([gc[-j % Q][T] for j in range(Q)], 1)
                block = gw[-i % Q][T].astype(F32)
            scores = jnp.dot(block.T.astype(BF16), panel, preferred_element_type=F32)
            p, h = entropy(scores)
            if t > 0:
                m = 0.5 * (p_ref[...] + p)
                rest = 1.0 - m
                mixed = m * jnp.log(jnp.maximum(m, tiny)) + rest * jnp.log(jnp.maximum(rest, tiny))
                js = 0.5 * (h_ref[...] + h) - mixed
                total = js[:, :B] + js[:, B : 2 * B] + js[:, 2 * B : 3 * B] + js[:, 3 * B :]
                total = jnp.sum(total.T, axis=0, keepdims=True)
                high = total.astype(BF16).astype(F32)
                out_ref[t - 1, :, i * B : (i + 1) * B] = jnp.where(
                    row == 0, high, jnp.where(row == 1, total - high, 0.0)
                )
            if t < T:
                p_ref[...] = p
                h_ref[...] = h


def drift_parts(n, c, gw, gc):
    return pl.pallas_call(
        drift_kernel,
        in_specs=[vmem()] * (4 * Q),
        out_specs=vmem(),
        out_shape=sds((T, 8, Q * B), F32),
        scratch_shapes=[pltpu.VMEM((B, Q * B), F32)] * 2,
        compiler_params=PARAMS(),
        cost_estimate=cost(2 * 5 * 512 * 512 * (EP + 30), 4 << 20, 5 * 5 * 512 * 512),
        name="drift",
    )(*n, *c, *gw, *gc)


NEAR_FIRST = (0, 1, 3, 2)


def summary_kernel(drift, *refs):
    parts = ([refs[2 * i] for i in NEAR_FIRST], [refs[2 * i + 1] for i in NEAR_FIRST])
    co_ref, b_ref, own_ref = refs[2 * Q : 2 * Q + 3]
    for q in range(2):
        for t in range(T):
            total = parts[q][0][t].astype(F32)
            for r in parts[q][1:]:
                total = total + r[t].astype(F32)
            if drift and q == 0:
                refs[-1][t : t + 1] = total[E : E + 1] + total[E + 1 : E + 2]
            total = total[:E]
            b_ref[q, t] = total
        forward = b_ref[q, 0]
        for t in range(1, T):
            forward = b_ref[q, t] + co_ref[t : t + 1] * forward
        backward = b_ref[q, T - 1]
        for t in reversed(range(T - 1)):
            backward = b_ref[q, t] + co_ref[T + t : T + t + 1] * backward
        own_ref[q] = forward.astype(BF16)
        own_ref[2 + q] = backward.astype(BF16)


def summaries(gw, gc, co, drift):
    return pl.pallas_call(
        functools.partial(summary_kernel, drift),
        in_specs=[vmem()] * (2 * Q + 1),
        out_specs=[vmem()] * (2 + drift),
        out_shape=[sds((2, T, E, B), F32), sds((4, E, B), BF16)] + [sds((T, B), F32)] * drift,
        compiler_params=PARAMS(),
        cost_estimate=cost(2 * T * EP * B * 10, 3 << 20),
        name="summaries",
    )(*[side[s] for s in NEAR_FIRST for side in (gw, gc)], co)


def chip_kernel(own_ref, other_ref, co_ref, *outs):
    k = lax.axis_index("tm")
    even, z = k % 2 == 0, k // 2
    chips = 2 * HALF
    for q in range(2):
        own, other = own_ref[q].astype(F32), other_ref[q].astype(F32)
        forward = jnp.where(even, other, own) + co_ref[12:13] * jnp.where(even, own, other)
        own, other = own_ref[2 + q].astype(F32), other_ref[2 + q].astype(F32)
        backward = jnp.where(even, own, other) + co_ref[13:14] * jnp.where(even, other, own)
        for d in range(1, HALF):
            is_forward = jnp.where(even, z + d < chips, z < d)
            outs[d - 1][q] = jnp.where(is_forward, forward, backward).astype(BF16)

        @pl.when(k % 2 == q)
        def _():
            outs[HALF - 1][...] = jnp.where(z < HALF, forward, backward).astype(BF16)


def chip_summaries(own, other, co):
    return pl.pallas_call(
        chip_kernel,
        in_specs=[vmem()] * 3,
        out_specs=[vmem()] * HALF,
        out_shape=[sds((2, E, B), BF16)] * (HALF - 1) + [sds((E, B), BF16)],
        compiler_params=PARAMS(),
        cost_estimate=cost(EP * B * 16, 1 << 20),
        name="chip_summaries",
    )(own, other, co)


def incoming_kernel(*refs):
    got, co_ref, out_ref = refs[:HALF][::-1], refs[HALF], refs[HALF + 1]
    core = lax.axis_index("tm") % 2
    for q in range(2):
        for way in range(2):
            row = 16 + 4 * way
            total = co_ref[row : row + 1] * got[0][q].astype(F32)
            for d in range(2, HALF):
                total = total + co_ref[row + d - 1 : row + d] * got[d - 1][q].astype(F32)
            across = co_ref[row + HALF - 1 : row + HALF] * got[HALF - 1][...].astype(F32)
            total = total + jnp.where(core == q, across, jnp.zeros_like(across))
            out_ref[2 * way + q] = total.astype(BF16)


def incoming(got, co):
    return pl.pallas_call(
        incoming_kernel,
        in_specs=[vmem()] * (HALF + 1),
        out_specs=vmem(),
        out_shape=sds((4, E, B), BF16),
        compiler_params=PARAMS(),
        cost_estimate=cost(4 * EP * B * 8, 1 << 20),
        name="incoming",
    )(*got[::-1], co)


def entering(odd, q, near_ref, mine_ref, other_ref, co_ref):
    y = mine_ref[q].astype(F32) + other_ref[q].astype(F32)
    z = mine_ref[2 + q].astype(F32) + other_ref[2 + q].astype(F32)
    y_odd = near_ref[q].astype(F32) + co_ref[14:15] * y
    z_even = near_ref[2 + q].astype(F32) + co_ref[15:16] * z
    return jnp.where(odd, y_odd, y), jnp.where(odd, z, z_even)


def solved_years(b_ref, q, y, z, co_ref):
    ys = []
    for t in range(T):
        y = b_ref[q, t] + co_ref[t : t + 1] * y
        ys.append(y)
    out = [None] * T
    for t in reversed(range(T)):
        carried = co_ref[T + t : T + t + 1] * z
        z = b_ref[q, t] + carried
        out[t] = (ys[t] + carried) * co_ref[2 * T + t : 2 * T + t + 1]
    return out


def update_kernel(scale, b_ref, near_ref, mine_ref, other_ref, co_ref, w_ref, c_ref, *refs):
    odd = lax.axis_index("tm") % 2 == 1
    for q, (old, new) in enumerate(((w_ref, refs[-2]), (c_ref, refs[-1]))):
        y, z = entering(odd, q, near_ref, mine_ref, other_ref, co_ref)
        solved = solved_years(b_ref, q, y, z, co_ref)
        for t in range(T):
            new[t] = (old[t].astype(F32) + scale * solved[t]).astype(BF16)


def finish_kernel(scale, vocab, *refs):
    *ins, raw_ref, nw_ref, nc_ref, drift_ref = refs
    update_kernel(scale, *ins, nw_ref, nc_ref)
    last = lax.axis_index("tm") == lax.axis_size("tm") - 1
    drift = raw_ref[...] * (float(vocab) ** -0.5)
    at = lax.broadcasted_iota(jnp.int32, (T, B), 0)
    drift_ref[...] = jnp.where(jnp.logical_and(last, at == T - 1), 0.0, drift)


def update(scale, *arrays):
    return pl.pallas_call(
        functools.partial(update_kernel, scale),
        in_specs=[vmem()] * 7,
        out_specs=[vmem()] * 2,
        out_shape=[sds((T, E, B), BF16)] * 2,
        compiler_params=PARAMS(),
        cost_estimate=cost(2 * T * EP * B * 10, 3 << 20),
        name="update",
    )(*arrays)


def finish(scale, vocab, *arrays):
    return pl.pallas_call(
        functools.partial(finish_kernel, scale, vocab),
        in_specs=[vmem()] * 8,
        out_specs=[vmem()] * 3,
        out_shape=[sds((T, E, B), BF16)] * 2 + [sds((T, B), F32)],
        compiler_params=PARAMS(),
        cost_estimate=cost(2 * T * EP * B * 10, 3 << 20),
        name="finish",
    )(*arrays)


def step(v, s, rows):
    y, x = v // Q, v % Q
    return y * Q + (x + s) % Q if rows else ((y + s) % Q) * Q + x


def in_grid(a, s, of_words):
    years, places = lax.axis_size("tm"), Q * Q
    pairs = [
        (k * places + v, k * places + step(v, s, (k % 2 == 0) == of_words))
        for k in range(years)
        for v in range(places)
    ]
    return lax.ppermute(a, ("tm", "vocab"), pairs)


def other_core(a):
    return lax.ppermute(a, "tm", [(k, k ^ 1) for k in range(lax.axis_size("tm"))])


def along_z(a, d):
    chips = lax.axis_size("tm") // 2
    ahead = [(2 * z, 2 * ((z + d) % chips)) for z in range(chips)]
    back = [(2 * z + 1, 2 * ((z - d) % chips) + 1) for z in range(chips)]
    return lax.ppermute(a, "tm", ahead + back)


def from_next(a):
    return lax.ppermute(a, "tm", [(k, k - 1) for k in range(1, lax.axis_size("tm"))])


ORDER = (1, 2, 3)


def spread(words, contexts):
    w, c = {0: words[0]}, {0: contexts[0]}
    for s in ORDER:
        w[s] = in_grid(words[s], s, True)
        c[s] = in_grid(contexts[s], s, False)
    return [w[s] for s in range(Q)], [c[s] for s in range(Q)]


def collected(words, contexts):
    w, c = {0: words[0]}, {0: contexts[0]}
    for s in ORDER:
        w[s] = in_grid(words[s], -s, True)
        c[s] = in_grid(contexts[s], -s, False)
    return [w[s] for s in range(Q)], [c[s] for s in range(Q)]


def on_device(counts, word_vecs, ctx_vecs, gaps):
    vocab = counts.shape[2]
    scale = RATE / float(vocab) ** 0.5
    words, contexts = word_vecs.transpose(0, 2, 1), ctx_vecs.transpose(0, 2, 1)
    loads = stage(counts, words)
    n, c = spread(loads, [contexts] * Q)
    held, c[1] = lax.optimization_barrier((jnp.stack([words[0], contexts[0]], 0), c[1]))
    following = from_next(held)
    co = coefficients(gaps)
    w, extra = (), following
    for sweep in range(SWEEPS):
        last = sweep == SWEEPS - 1
        if sweep:
            w, c = spread([words] * Q, [contexts] * Q)
        grads = gradients(n, c, extra, w)
        gw, gc = collected(grads[:Q], grads[Q:])
        b, own, *raw = summaries(gw, gc, co, last)
        near = other_core(own)
        outs = chip_summaries(own, near, co)
        if sweep == 0:
            outs, held = lax.optimization_barrier((outs, c))
            extra = drift_parts(n, held, gw, gc)
        got = {d: along_z(outs[d - 1], d) for d in (4, 3, 2, 1)}
        got = [got[d] for d in range(1, HALF + 1)]
        if sweep == 0:
            extra, *got = lax.optimization_barrier((extra, *got[::-1]))
            got = got[::-1]
        mine = incoming(got, co)
        other = other_core(mine)
        if last:
            words, contexts, drift = finish(
                scale, vocab, b, near, mine, other, co, words, contexts, *raw
            )
            return (words.transpose(0, 2, 1), contexts.transpose(0, 2, 1), drift)
        words, contexts = update(scale, b, near, mine, other, co, words, contexts)


def solution(mesh):
    return jax.shard_map(
        on_device,
        mesh=mesh,
        in_specs=(P("tm", "vocab", None), P("tm", "vocab", None), P("tm", "vocab", None), P()),
        out_specs=(P("tm", "vocab", None), P("tm", "vocab", None), P("tm", "vocab")),
        check_vma=False,
    )
```

```python
import functools

import jax
import jax.numpy as jnp
from jax import lax
from jax.experimental import pallas as pl
from jax.experimental.pallas import tpu as pltpu
from jax.sharding import PartitionSpec as P

PRIOR = 0.05
DIFF = 0.5
RATE = 0.2
SWEEPS = 2


E = 200
EP = 208
B = 128
T = 4
Q = 4
HALF = 4
F32 = jnp.float32
BF16 = jnp.bfloat16

PARAMS = functools.partial(pltpu.CompilerParams, vmem_limit_bytes=24 * 1024 * 1024)


def sds(shape, dtype):
    return jax.ShapeDtypeStruct(shape, dtype)


def vmem():
    return pl.BlockSpec(memory_space=pltpu.VMEM)


def cost(flops, moved, special=0):
    return pl.CostEstimate(flops=int(flops), bytes_accessed=int(moved), transcendentals=int(special))


COUNT_ROWS = T * Q * B
ROWS = COUNT_ROWS + T * EP


def count_block(ref, t, j):
    at = (t * Q + j) * B
    return ref[at : at + B]


def word_block(ref, t):
    at = COUNT_ROWS + t * EP
    return ref[at : at + EP]


def stage_kernel(counts_ref, w_ref, *loads):
    along_rows = lax.axis_index("tm") % 2 == 0
    place = lax.axis_index("vocab")
    y, x = place // Q, place % Q
    row = lax.broadcasted_iota(jnp.int32, (8, B), 0)
    ones = jnp.ones((8, B), BF16)
    for t in range(T):
        total = jnp.zeros((8, B), F32)
        for s in range(Q):
            for j in range(Q):
                block = jnp.where(
                    along_rows,
                    ((y + Q - j) % Q) * Q + (x + s) % Q,
                    ((y + s) % Q) * Q + (x + Q - j) % Q,
                )
                at = pl.multiple_of(block * B, B)
                to = (t * Q + j) * B
                part = counts_ref[t, :, pl.ds(at, B)].astype(F32).astype(BF16)
                loads[s][to : to + B] = part
                total = total + lax.dot_general(
                    ones, part, (((1,), (1,)), ((), ())), preferred_element_type=F32
                )
        high = total.astype(BF16).astype(F32)
        spare = jnp.where(row == 0, high, jnp.where(row == 1, total - high, 0.0))
        word = jnp.concatenate([w_ref[t].astype(F32), spare], 0).astype(BF16)
        for s in range(Q):
            loads[s][COUNT_ROWS + t * EP : COUNT_ROWS + (t + 1) * EP] = word


def stage(counts, words):
    vocab = counts.shape[2]
    return pl.pallas_call(
        stage_kernel,
        in_specs=[vmem()] * 2,
        out_specs=[vmem()] * Q,
        out_shape=[sds((ROWS, B), BF16)] * Q,
        compiler_params=PARAMS(),
        cost_estimate=cost(T * B * vocab * 16, T * B * vocab * 6),
        name="stage",
    )(counts, words)


def coefficient_kernel(gaps_ref, out_ref, link_ref, f_ref, g_ref, d_ref, e_ref, a_ref, c_ref):
    years = gaps_ref.shape[0]
    chips = years // (2 * T)
    one = jnp.ones((1, B), F32)
    zero = jnp.zeros((1, B), F32)
    for t in range(years - 1):
        link_ref[t : t + 1] = one / (DIFF * (one * gaps_ref[t].astype(F32)))

    def link(t):
        return link_ref[t : t + 1] if 0 <= t < years - 1 else zero

    def diagonal(t):
        return PRIOR + link(t - 1) + link(t)

    delta, eps = diagonal(0), diagonal(years - 1)
    f_ref[0:1] = zero
    g_ref[years - 1 : years] = zero
    d_ref[0:1] = delta
    e_ref[years - 1 : years] = eps
    for t in range(1, years):
        f = link(t - 1) / delta
        delta = diagonal(t) - link(t - 1) * f
        f_ref[t : t + 1] = f
        d_ref[t : t + 1] = delta
        u = years - 1 - t
        g = link(u) / eps
        eps = diagonal(u) - link(u) * g
        g_ref[u : u + 1] = g
        e_ref[u : u + 1] = eps
    for t in range(years):
        d_ref[t : t + 1] = one / (d_ref[t : t + 1] + e_ref[t : t + 1] - diagonal(t))
    for k in range(2 * chips):
        fs, gs = f_ref[k * T : k * T + 1], g_ref[k * T : k * T + 1]
        for j in range(1, T):
            fs = fs * f_ref[k * T + j : k * T + j + 1]
            gs = gs * g_ref[k * T + j : k * T + j + 1]
        a_ref[k : k + 1] = fs
        c_ref[k : k + 1] = gs
    k = lax.axis_index("tm")
    z = k // 2
    for j in range(T):
        out_ref[j : j + 1] = f_ref[pl.ds(k * T + j, 1)]
        out_ref[T + j : T + j + 1] = g_ref[pl.ds(k * T + j, 1)]
        out_ref[2 * T + j : 2 * T + j + 1] = d_ref[pl.ds(k * T + j, 1)]
    out_ref[12:13] = a_ref[pl.ds(2 * z + 1, 1)]
    out_ref[13:14] = c_ref[pl.ds(2 * z, 1)]
    out_ref[14:15] = a_ref[pl.ds(2 * z, 1)]
    out_ref[15:16] = c_ref[pl.ds(2 * z + 1, 1)]
    forward, backward = one, one
    earliest, latest = {}, {}
    for d in range(1, chips):
        earliest[d], latest[d] = forward, backward
        before = jnp.maximum(z - d, 0)
        after = jnp.minimum(z + d, chips - 1)
        forward = forward * a_ref[pl.ds(2 * before, 1)] * a_ref[pl.ds(2 * before + 1, 1)]
        backward = backward * c_ref[pl.ds(2 * after, 1)] * c_ref[pl.ds(2 * after + 1, 1)]
    ahead = k % 2 == 0
    for d in range(1, HALF + 1):
        whole = chips - d
        is_forward = jnp.where(jnp.logical_or(ahead, d == HALF), z >= d, z + d >= chips)
        weight = jnp.where(
            jnp.logical_or(ahead, d == HALF),
            jnp.where(is_forward, earliest[d], latest[whole]),
            jnp.where(is_forward, earliest[whole], latest[d]),
        )
        out_ref[15 + d : 16 + d] = jnp.where(is_forward, weight, zero)
        out_ref[19 + d : 20 + d] = jnp.where(is_forward, zero, weight)


def coefficients(gaps):
    years = gaps.shape[0]
    return pl.pallas_call(
        coefficient_kernel,
        in_specs=[pl.BlockSpec(memory_space=pltpu.SMEM)],
        out_specs=vmem(),
        out_shape=sds((24, B), F32),
        scratch_shapes=[pltpu.VMEM((years, B), F32)] * 5 + [pltpu.VMEM((16, B), F32)] * 2,
        compiler_params=PARAMS(),
        cost_estimate=cost(years * B * 200, years * 600),
        name="coefficients",
    )(gaps)


def gradient_kernel(first, *refs):
    n, c, extra = refs[:Q], refs[Q : 2 * Q], refs[2 * Q]
    refs = refs[2 * Q + 1 :]
    if not first:
        w, refs = refs[:Q], refs[Q:]
    gw, gc, coeff_ref = refs[:Q], refs[Q : 2 * Q], refs[2 * Q]
    vocab = Q * Q * B
    for t in range(T):
        panel = jnp.concatenate([r[t] for r in c], 1)
        words = []
        for i in range(Q):
            loaded = word_block(n[i], t).astype(F32)
            block = loaded[:E] if first else w[i][t].astype(F32)
            words.append(block.astype(BF16))
            spare = loaded[E:].T
            negative = (spare[:, 0:1] + spare[:, 1:2]) * (1.0 / vocab)
            scores = jnp.dot(block.T.astype(BF16), panel, preferred_element_type=F32)
            weights = jnp.concatenate([count_block(n[i], t, j) for j in range(Q)], 1).astype(F32)
            half = jnp.tanh(0.5 * scores)
            coeff = 0.5 * ((weights - negative) - (weights + negative) * half)
            coeff_ref[t % 2, i * B : (i + 1) * B, :] = coeff.astype(BF16)
        coeff = coeff_ref[t % 2]
        word_grad = lax.dot_general(
            panel, coeff, (((1,), (1,)), ((), ())), preferred_element_type=F32
        )
        ctx_grad = jnp.dot(jnp.concatenate(words, 1), coeff, preferred_element_type=F32)
        if not first:
            word_grad = jnp.concatenate([word_grad, extra[t]], 0)
            ctx_grad = jnp.concatenate([ctx_grad, jnp.zeros_like(extra[t])], 0)
        word_grad, ctx_grad = word_grad.astype(BF16), ctx_grad.astype(BF16)
        for i in range(Q):
            gw[i][t] = word_grad[:, i * B : (i + 1) * B]
            gc[i][t] = ctx_grad[:, i * B : (i + 1) * B]
    if first:
        for i in range(Q):
            gw[i][T] = extra[0]
            gc[i][T] = extra[1]


def gradients(n, c, extra, w=()):
    first = not w
    return pl.pallas_call(
        functools.partial(gradient_kernel, first),
        in_specs=[vmem()] * (2 * Q + 1 + len(w)),
        out_specs=[vmem()] * (2 * Q),
        out_shape=[sds((T + first, E if first else EP, B), BF16)] * (2 * Q),
        scratch_shapes=[pltpu.VMEM((2, Q * B, Q * B), BF16)],
        compiler_params=PARAMS(),
        cost_estimate=cost(6 * T * 512 * 512 * EP, 6 << 20, 2 * T * 512 * 512),
        name="gradients",
    )(*n, *c, extra, *w)


def entropy(scores):
    size = jnp.abs(scores)
    small = jnp.exp(-size)
    upper = 1.0 / (1.0 + small)
    lower = small * upper
    return jnp.where(scores >= 0, upper, lower), jnp.log(upper) - lower * size


def drift_kernel(*refs):
    n, c, gw, gc = (refs[i * Q : (i + 1) * Q] for i in range(4))
    out_ref, p_ref, h_ref = refs[4 * Q :]
    tiny = jnp.finfo(F32).tiny
    row = lax.broadcasted_iota(jnp.int32, (8, B), 0)
    for i in range(Q):
        for t in range(T + 1):
            if t < T:
                panel = jnp.concatenate([r[t] for r in c], 1)
                block = word_block(n[i], t).astype(F32)[:E]
            else:
                panel = jnp.concatenate([gc[-j % Q][T] for j in range(Q)], 1)
                block = gw[-i % Q][T].astype(F32)
            scores = jnp.dot(block.T.astype(BF16), panel, preferred_element_type=F32)
            p, h = entropy(scores)
            if t > 0:
                m = 0.5 * (p_ref[...] + p)
                rest = 1.0 - m
                mixed = m * jnp.log(jnp.maximum(m, tiny)) + rest * jnp.log(jnp.maximum(rest, tiny))
                js = 0.5 * (h_ref[...] + h) - mixed
                total = js[:, :B] + js[:, B : 2 * B] + js[:, 2 * B : 3 * B] + js[:, 3 * B :]
                total = jnp.sum(total.T, axis=0, keepdims=True)
                high = total.astype(BF16).astype(F32)
                out_ref[t - 1, :, i * B : (i + 1) * B] = jnp.where(
                    row == 0, high, jnp.where(row == 1, total - high, 0.0)
                )
            if t < T:
                p_ref[...] = p
                h_ref[...] = h


def drift_parts(n, c, gw, gc):
    return pl.pallas_call(
        drift_kernel,
        in_specs=[vmem()] * (4 * Q),
        out_specs=vmem(),
        out_shape=sds((T, 8, Q * B), F32),
        scratch_shapes=[pltpu.VMEM((B, Q * B), F32)] * 2,
        compiler_params=PARAMS(),
        cost_estimate=cost(2 * 5 * 512 * 512 * (EP + 30), 4 << 20, 5 * 5 * 512 * 512),
        name="drift",
    )(*n, *c, *gw, *gc)


NEAR_FIRST = (0, 1, 3, 2)


def summary_kernel(drift, *refs):
    parts = ([refs[2 * i] for i in NEAR_FIRST], [refs[2 * i + 1] for i in NEAR_FIRST])
    co_ref, b_ref, own_ref = refs[2 * Q : 2 * Q + 3]
    for q in range(2):
        for t in range(T):
            total = parts[q][0][t].astype(F32)
            for r in parts[q][1:]:
                total = total + r[t].astype(F32)
            if drift and q == 0:
                refs[-1][t : t + 1] = total[E : E + 1] + total[E + 1 : E + 2]
            total = total[:E]
            b_ref[q, t] = total
        forward = b_ref[q, 0]
        for t in range(1, T):
            forward = b_ref[q, t] + co_ref[t : t + 1] * forward
        backward = b_ref[q, T - 1]
        for t in reversed(range(T - 1)):
            backward = b_ref[q, t] + co_ref[T + t : T + t + 1] * backward
        own_ref[q] = forward.astype(BF16)
        own_ref[2 + q] = backward.astype(BF16)


def summaries(gw, gc, co, drift):
    return pl.pallas_call(
        functools.partial(summary_kernel, drift),
        in_specs=[vmem()] * (2 * Q + 1),
        out_specs=[vmem()] * (2 + drift),
        out_shape=[sds((2, T, E, B), F32), sds((4, E, B), BF16)] + [sds((T, B), F32)] * drift,
        compiler_params=PARAMS(),
        cost_estimate=cost(2 * T * EP * B * 10, 3 << 20),
        name="summaries",
    )(*[side[s] for s in NEAR_FIRST for side in (gw, gc)], co)


def chip_kernel(own_ref, other_ref, co_ref, *outs):
    k = lax.axis_index("tm")
    even, z = k % 2 == 0, k // 2
    chips = 2 * HALF
    for q in range(2):
        own, other = own_ref[q].astype(F32), other_ref[q].astype(F32)
        forward = jnp.where(even, other, own) + co_ref[12:13] * jnp.where(even, own, other)
        own, other = own_ref[2 + q].astype(F32), other_ref[2 + q].astype(F32)
        backward = jnp.where(even, own, other) + co_ref[13:14] * jnp.where(even, other, own)
        for d in range(1, HALF):
            is_forward = jnp.where(even, z + d < chips, z < d)
            outs[d - 1][q] = jnp.where(is_forward, forward, backward).astype(BF16)

        @pl.when(k % 2 == q)
        def _():
            outs[HALF - 1][...] = jnp.where(z < HALF, forward, backward).astype(BF16)


def chip_summaries(own, other, co):
    return pl.pallas_call(
        chip_kernel,
        in_specs=[vmem()] * 3,
        out_specs=[vmem()] * HALF,
        out_shape=[sds((2, E, B), BF16)] * (HALF - 1) + [sds((E, B), BF16)],
        compiler_params=PARAMS(),
        cost_estimate=cost(EP * B * 16, 1 << 20),
        name="chip_summaries",
    )(own, other, co)


def incoming_kernel(*refs):
    got, co_ref, out_ref = refs[:HALF][::-1], refs[HALF], refs[HALF + 1]
    core = lax.axis_index("tm") % 2
    for q in range(2):
        for way in range(2):
            row = 16 + 4 * way
            total = co_ref[row : row + 1] * got[0][q].astype(F32)
            for d in range(2, HALF):
                total = total + co_ref[row + d - 1 : row + d] * got[d - 1][q].astype(F32)
            across = co_ref[row + HALF - 1 : row + HALF] * got[HALF - 1][...].astype(F32)
            total = total + jnp.where(core == q, across, jnp.zeros_like(across))
            out_ref[2 * way + q] = total.astype(BF16)


def incoming(got, co):
    return pl.pallas_call(
        incoming_kernel,
        in_specs=[vmem()] * (HALF + 1),
        out_specs=vmem(),
        out_shape=sds((4, E, B), BF16),
        compiler_params=PARAMS(),
        cost_estimate=cost(4 * EP * B * 8, 1 << 20),
        name="incoming",
    )(*got[::-1], co)


def entering(odd, q, near_ref, mine_ref, other_ref, co_ref):
    y = mine_ref[q].astype(F32) + other_ref[q].astype(F32)
    z = mine_ref[2 + q].astype(F32) + other_ref[2 + q].astype(F32)
    y_odd = near_ref[q].astype(F32) + co_ref[14:15] * y
    z_even = near_ref[2 + q].astype(F32) + co_ref[15:16] * z
    return jnp.where(odd, y_odd, y), jnp.where(odd, z, z_even)


def solved_years(b_ref, q, y, z, co_ref):
    ys = []
    for t in range(T):
        y = b_ref[q, t] + co_ref[t : t + 1] * y
        ys.append(y)
    out = [None] * T
    for t in reversed(range(T)):
        carried = co_ref[T + t : T + t + 1] * z
        z = b_ref[q, t] + carried
        out[t] = (ys[t] + carried) * co_ref[2 * T + t : 2 * T + t + 1]
    return out


def update_kernel(scale, b_ref, near_ref, mine_ref, other_ref, co_ref, w_ref, c_ref, *refs):
    odd = lax.axis_index("tm") % 2 == 1
    for q, (old, new) in enumerate(((w_ref, refs[-2]), (c_ref, refs[-1]))):
        y, z = entering(odd, q, near_ref, mine_ref, other_ref, co_ref)
        solved = solved_years(b_ref, q, y, z, co_ref)
        for t in range(T):
            new[t] = (old[t].astype(F32) + scale * solved[t]).astype(BF16)


def finish_kernel(scale, vocab, *refs):
    *ins, raw_ref, nw_ref, nc_ref, drift_ref = refs
    update_kernel(scale, *ins, nw_ref, nc_ref)
    last = lax.axis_index("tm") == lax.axis_size("tm") - 1
    drift = raw_ref[...] * (float(vocab) ** -0.5)
    at = lax.broadcasted_iota(jnp.int32, (T, B), 0)
    drift_ref[...] = jnp.where(jnp.logical_and(last, at == T - 1), 0.0, drift)


def update(scale, *arrays):
    return pl.pallas_call(
        functools.partial(update_kernel, scale),
        in_specs=[vmem()] * 7,
        out_specs=[vmem()] * 2,
        out_shape=[sds((T, E, B), BF16)] * 2,
        compiler_params=PARAMS(),
        cost_estimate=cost(2 * T * EP * B * 10, 3 << 20),
        name="update",
    )(*arrays)


def finish(scale, vocab, *arrays):
    return pl.pallas_call(
        functools.partial(finish_kernel, scale, vocab),
        in_specs=[vmem()] * 8,
        out_specs=[vmem()] * 3,
        out_shape=[sds((T, E, B), BF16)] * 2 + [sds((T, B), F32)],
        compiler_params=PARAMS(),
        cost_estimate=cost(2 * T * EP * B * 10, 3 << 20),
        name="finish",
    )(*arrays)


def step(v, s, rows):
    y, x = v // Q, v % Q
    return y * Q + (x + s) % Q if rows else ((y + s) % Q) * Q + x


def in_grid(a, s, of_words):
    years, places = lax.axis_size("tm"), Q * Q
    pairs = [
        (k * places + v, k * places + step(v, s, (k % 2 == 0) == of_words))
        for k in range(years)
        for v in range(places)
    ]
    return lax.ppermute(a, ("tm", "vocab"), pairs)


def other_core(a):
    return lax.ppermute(a, "tm", [(k, k ^ 1) for k in range(lax.axis_size("tm"))])


def along_z(a, d):
    chips = lax.axis_size("tm") // 2
    ahead = [(2 * z, 2 * ((z + d) % chips)) for z in range(chips)]
    back = [(2 * z + 1, 2 * ((z - d) % chips) + 1) for z in range(chips)]
    return lax.ppermute(a, "tm", ahead + back)


def from_next(a):
    return lax.ppermute(a, "tm", [(k, k - 1) for k in range(1, lax.axis_size("tm"))])


ORDER = (1, 2, 3)


def spread(words, contexts):
    w, c = {0: words[0]}, {0: contexts[0]}
    for s in ORDER:
        w[s] = in_grid(words[s], s, True)
        c[s] = in_grid(contexts[s], s, False)
    return [w[s] for s in range(Q)], [c[s] for s in range(Q)]


def collected(words, contexts):
    w, c = {0: words[0]}, {0: contexts[0]}
    for s in ORDER:
        w[s] = in_grid(words[s], -s, True)
        c[s] = in_grid(contexts[s], -s, False)
    return [w[s] for s in range(Q)], [c[s] for s in range(Q)]


def on_device(counts, word_vecs, ctx_vecs, gaps):
    vocab = counts.shape[2]
    scale = RATE / float(vocab) ** 0.5
    words, contexts = word_vecs.transpose(0, 2, 1), ctx_vecs.transpose(0, 2, 1)
    loads = stage(counts, words)
    n, c = spread(loads, [contexts] * Q)
    held, c[3] = lax.optimization_barrier((jnp.stack([words[0], contexts[0]], 0), c[3]))
    following = from_next(held)
    co = coefficients(gaps)
    w, extra = (), following
    for sweep in range(SWEEPS):
        last = sweep == SWEEPS - 1
        if sweep:
            w, c = spread([words] * Q, [contexts] * Q)
        grads = gradients(n, c, extra, w)
        gw, gc = collected(grads[:Q], grads[Q:])
        b, own, *raw = summaries(gw, gc, co, last)
        near = other_core(own)
        outs = chip_summaries(own, near, co)
        if sweep == 0:
            outs, held = lax.optimization_barrier((outs, c))
            extra = drift_parts(n, held, gw, gc)
        got = {d: along_z(outs[d - 1], d) for d in (4, 3, 2, 1)}
        got = [got[d] for d in range(1, HALF + 1)]
        if sweep == 0:
            extra, *got = lax.optimization_barrier((extra, *got[::-1]))
            got = got[::-1]
        mine = incoming(got, co)
        other = other_core(mine)
        if last:
            words, contexts, drift = finish(
                scale, vocab, b, near, mine, other, co, words, contexts, *raw
            )
            return (words.transpose(0, 2, 1), contexts.transpose(0, 2, 1), drift)
        words, contexts = update(scale, b, near, mine, other, co, words, contexts)


def solution(mesh):
    return jax.shard_map(
        on_device,
        mesh=mesh,
        in_specs=(P("tm", "vocab", None), P("tm", "vocab", None), P("tm", "vocab", None), P()),
        out_specs=(P("tm", "vocab", None), P("tm", "vocab", None), P("tm", "vocab")),
        check_vma=False,
    )
```
